256 devices in a mesh: dp: 64 (over y, x_lo, z), layer: 4 (over x_hi, core).
Axes of the slice: x: 4 (x_hi: 2, x_lo: 2; x = x_hi * 2 + x_lo), y: 4, z: 8, core: 2. Of those that a mesh axis runs over, the one named last changes fastest.
Arguments:
- train_acts: bfloat16 [4, 16384, 4096], P('layer', 'dp'), may hold values from -6 to 6
- train_grads: bfloat16 [4, 16384, 14336], P('layer', 'dp'), may hold values from -6 to 6
- query_acts: bfloat16 [4, 4096, 4096], P('layer', 'dp'), may hold values from -6 to 6
- query_grads: bfloat16 [4, 4096, 14336], P('layer', 'dp'), may hold values from -6 to 6
- basis_out: bfloat16 [4, 14336, 64], P('layer', 'dp'), may hold values from -0.046875 to 0.046875
- basis_in: bfloat16 [4, 4096, 64], P('layer', 'dp'), may hold values from -0.09375 to 0.09375
- eigvals: float32 [4, 64, 64], P('layer'), may hold values from 0.1 to 10
Outputs:
- scores: float32 [64, 128], P(None, 'dp')
The draws below stay inside these ranges and needn't reach their ends.
All inputs are finite; a program needn't handle non-finite values.
Results may differ from the reference program's by a relative error of at most 0.02.
Values may be sent and summed in bfloat16 or wider, within the bound.
A program may use at most 128 MiB of HBM per device.

```python
import math
import jax
import jax.numpy as jnp

D = 4096
FF = 14336
R = 64
SEQ = 128
QSEQ = 64
LAYERS = 4
TRAIN = 128
QUERIES = 64


def block_levels(stream_key, shape, cuts, smallest, largest):
    def one(position, shards_of):
        heights = jax.random.uniform(jax.random.fold_in(jax.random.fold_in(stream_key, 6), position), (shards_of,), jnp.float32, smallest / len(cuts), largest / len(cuts))
        return jnp.repeat(jnp.exp(heights), shape[position] // shards_of).reshape((-1,) + (1,) * (len(shape) - position - 1))

    loudness = one(*cuts[0])
    for cut in cuts[1:]:
        loudness = loudness * one(*cut)
    return loudness


def centred(own_key, dims, width, limit, pieces=(), dtype=jnp.bfloat16):
    result = width * jax.random.normal(own_key, dims, jnp.float32)
    if pieces:
        result = result * block_levels(own_key, dims, pieces, -0.22, 0.18)
    return jnp.clip(result, -limit, limit).astype(dtype)


def setup_inputs(seed: int = 0) -> dict:
    key_of = jax.random.split(jax.random.key(seed), 8)
    train_acts = centred(key_of[0], (LAYERS, TRAIN * SEQ, D), 1.0, 6.0, ((0, 4), (1, 64)))
    train_grads = centred(key_of[1], (LAYERS, TRAIN * SEQ, FF), 1.0, 6.0, ((0, 4), (1, 64)))
    query_acts = centred(key_of[2], (LAYERS, QUERIES * QSEQ, D), 1.0, 6.0, ((0, 4), (1, 64)))
    query_grads = centred(key_of[3], (LAYERS, QUERIES * QSEQ, FF), 1.0, 6.0, ((0, 4), (1, 64)))
    basis_out = centred(key_of[4], (LAYERS, FF, R), FF ** -0.5, 0.046875, ((0, 4), (1, 64)))
    basis_in = centred(key_of[5], (LAYERS, D, R), D ** -0.5, 0.09375, ((0, 4), (1, 64)))
    eigvals = jnp.clip(jnp.exp(math.log(10.0) - 4.6051702 * jax.random.uniform(key_of[6], (LAYERS, R, R), jnp.float32) ** block_levels(key_of[6], (LAYERS, R, R), ((0, 4),), -0.2, 0.2)), 0.1, 10.0)
    return dict(train_acts=train_acts, train_grads=train_grads, query_acts=query_acts, query_grads=query_grads, basis_out=basis_out, basis_in=basis_in, eigvals=eigvals)


def outer_mean(out_side, in_side, count, length):
    left = out_side.reshape(count, length, out_side.shape[1])
    right = in_side.reshape(count, length, in_side.shape[1])
    return jnp.einsum("esa,esb->eab", left, right) / length


def reference(train_acts, train_grads, query_acts, query_grads, basis_out, basis_in, eigvals):
    scores = jnp.zeros((QUERIES, TRAIN), jnp.float32)
    for level in range(LAYERS):
        train_out = jnp.dot(train_grads[level], basis_out[level], preferred_element_type=jnp.float32)
        train_in = jnp.dot(train_acts[level], basis_in[level], preferred_element_type=jnp.float32)
        query_out = jnp.dot(query_grads[level], basis_out[level], preferred_element_type=jnp.float32)
        query_in = jnp.dot(query_acts[level], basis_in[level], preferred_element_type=jnp.float32)
        train_proj = outer_mean(train_out, train_in, TRAIN, SEQ).reshape(TRAIN, R * R).astype(jnp.bfloat16)
        query_raw = outer_mean(query_out, query_in, QUERIES, QSEQ)
        query_pre = (query_raw / (eigvals[level] + 0.1)).reshape(QUERIES, R * R).astype(jnp.bfloat16)
        scores = scores + jnp.dot(query_pre, train_proj.T, preferred_element_type=jnp.float32)
    return scores
```

```python
import jax
import jax.numpy as jnp
from jax import lax
from jax.experimental import pallas as pl
from jax.experimental.pallas import tpu as pltpu
from jax.sharding import PartitionSpec as P

MESH = pl.DeviceIdType.MESH
NY, NX, NZ = 4, 2, 8
NP = NY * NX
NL = 4
OUT_ROWS, IN_ROWS = 224, 64
PACK_OUT, PACK_IN = OUT_ROWS // 2, IN_ROWS // 2
PACK = PACK_OUT + PACK_IN
SPLIT = 80
PARTS = ((0, SPLIT), (SPLIT, PACK - SPLIT))
BLOCK_OUT, BLOCK_IN = OUT_ROWS * NZ, IN_ROWS * NZ
TOK_Q, TOK_T = 64, 256
TOK = TOK_Q + TOK_T


def kernel(
    ta, tg, qa, qg, bo, bi, eig, out,
    a_in, a_out, b_o, b_i, eig_v, gath, w_out, w_in, acc_out, acc_in,
    sb1, rb1, qa_all, sb3, rb3,
    load_sem, act_sem, gsend, grecv, s1, r1, s2, r2, s3, r3,
):
    dp = lax.axis_index("dp")
    layer = lax.axis_index("layer")
    y = dp // 16
    x = lax.rem(dp // 8, 2)
    z = lax.rem(dp, 8)
    k = dp // 8
    x1 = 1 - x

    def dev(yy, xx, zz):
        return yy * 16 + xx * 8 + zz

    def ypeer(d):
        return lax.rem(y + d, NY)

    small = [
        pltpu.make_async_copy(bo.at[0], b_o, load_sem.at[0]),
        pltpu.make_async_copy(bi.at[0], b_i, load_sem.at[1]),
        pltpu.make_async_copy(eig.at[0], eig_v, load_sem.at[2]),
    ]
    for c in small:
        c.start()

    barrier = pltpu.get_barrier_semaphore()

    def greet_z(d, c):
        pl.semaphore_signal(
            barrier, inc=1, device_id=(dev(y, x, lax.rem(z + d, NZ)), layer), device_id_type=MESH
        )
        return c

    def greet_plane(d, c):
        kk = lax.rem(k + d // NL, NP)
        ll = lax.rem(layer + lax.rem(d, NL), NL)
        pl.semaphore_signal(barrier, inc=1, device_id=(kk * NZ + z, ll), device_id_type=MESH)
        return c

    lax.fori_loop(1, NZ, greet_z, 0)
    lax.fori_loop(1, NP * NL, greet_plane, 0)

    acts = [
        pltpu.make_async_copy(qa.at[0], a_in.at[pl.ds(0, TOK_Q)], act_sem.at[0]),
        pltpu.make_async_copy(ta.at[0], a_in.at[pl.ds(TOK_Q, TOK_T)], act_sem.at[1]),
        pltpu.make_async_copy(qg.at[0], a_out.at[pl.ds(0, TOK_Q)], act_sem.at[2]),
        pltpu.make_async_copy(tg.at[0], a_out.at[pl.ds(TOK_Q, TOK_T)], act_sem.at[3]),
    ]
    for c in acts:
        c.start()

    for c in small:
        c.wait()
    for t in range(PACK_OUT // 16):
        gath[dp, 16 * t : 16 * t + 16, :] = jnp.concatenate(
            [b_o[32 * t : 32 * t + 16, :], b_o[32 * t + 16 : 32 * t + 32, :]], axis=1
        )
    for t in range(PACK_IN // 16):
        gath[dp, PACK_OUT + 16 * t : PACK_OUT + 16 * t + 16, :] = jnp.concatenate(
            [b_i[32 * t : 32 * t + 16, :], b_i[32 * t + 16 : 32 * t + 32, :]], axis=1
        )

    pl.semaphore_wait(barrier, NZ - 1 + NP * NL - 1)

    def part_copy(j, part, to):
        start, size = PARTS[part]
        ref = gath.at[j, pl.ds(start, size)]
        return pltpu.make_async_remote_copy(
            src_ref=ref, dst_ref=ref, send_sem=gsend, recv_sem=grecv.at[part, j],
            device_id=(to, layer), device_id_type=MESH,
        )

    def arrived(j, part):
        part_copy(j, part, dp).wait_recv()

    def to_plane(j):
        for part in (0, 1):
            for d in (2, 1, 3):
                part_copy(j, part, dev(ypeer(d), x, z)).start()
            part_copy(j, part, dev(y, x1, z)).start()

    for d in (1, 7, 2, 6, 3, 5, 4):
        for part in (0, 1):
            part_copy(dp, part, dev(y, x, lax.rem(z + d, NZ))).start()
    to_plane(dp)

    def z_at(n):
        up = lax.rem(n, 2)
        off = (n + 1) // 2
        return lax.rem(z + NZ + off * (2 * up - 1), NZ)

    def first(n, c):
        j = dev(y, x, z_at(n))
        arrived(j, 0)
        arrived(j, 1)
        to_plane(j)
        return c

    def second(n, c):
        zz = z_at(n)
        j = dev(y, x1, zz)
        arrived(j, 1)
        for d in (2, 1, 3):
            part_copy(j, 1, dev(ypeer(d), x, z)).start()
        for d in (1, 3, 2):
            j = dev(ypeer(d), x, zz)
            arrived(j, 0)
            part_copy(j, 0, dev(y, x1, z)).start()
        return c

    def both(n, c):
        first(n, c)
        return second(n - 3, c)

    lax.fori_loop(1, 3, first, 0)
    lax.fori_loop(3, NZ, both, 0)
    lax.fori_loop(NZ - 3, NZ, second, 0)

    for c in acts:
        c.wait()
    acc_out[...] = jnp.zeros_like(acc_out)
    acc_in[...] = jnp.zeros_like(acc_in)
    low = lax.broadcasted_iota(jnp.int32, (16, 128), 1) < 64

    def block(yy, xx, parts):
        def unpack(zz, c):
            j = dev(yy, xx, zz)
            for part in parts:
                arrived(j, part)
            base = zz * OUT_ROWS
            for t in range(PACK_OUT // 16):
                tile = gath[j, 16 * t : 16 * t + 16, :]
                row = pl.multiple_of(base + 32 * t, 16)
                w_out[pl.ds(row, 16), :] = tile
                w_out[pl.ds(row + 16, 16), :] = jnp.concatenate(
                    [tile[:, 64:], tile[:, :64]], axis=1
                )
            base = zz * IN_ROWS
            for t in range(PACK_IN // 16):
                tile = gath[j, PACK_OUT + 16 * t : PACK_OUT + 16 * t + 16, :]
                row = pl.multiple_of(base + 32 * t, 16)
                turned = jnp.concatenate([tile[:, 64:], tile[:, :64]], axis=1)
                w_in[pl.ds(row, 16), :] = jnp.where(low, tile, turned)
                w_in[pl.ds(row + 16, 16), :] = jnp.where(low, turned, tile)
            return c

        lax.fori_loop(0, NZ, unpack, 0)
        kk = yy * NX + xx
        cols = pl.ds(pl.multiple_of(kk * BLOCK_IN, 128), BLOCK_IN)
        acc_in[...] += jnp.dot(a_in[:, cols], w_in[...], preferred_element_type=jnp.float32)
        cols = pl.ds(pl.multiple_of(kk * BLOCK_OUT, 128), BLOCK_OUT)
        acc_out[...] += jnp.dot(a_out[:, cols], w_out[...], preferred_element_type=jnp.float32)

    block(y, x, ())

    def same_x(d, c):
        block(ypeer(d), x, (1,))
        return c

    def other_x(d, c):
        block(ypeer(d), x1, (0, 1))
        return c

    lax.fori_loop(1, NY, same_x, 0)
    block(y, x1, (0,))
    lax.fori_loop(1, NY, other_x, 0)

    half = lax.broadcasted_iota(jnp.int32, (32, 128), 1) < 64

    def outer(start, length):
        left = acc_out[start : start + length, :].astype(jnp.bfloat16)
        right = acc_in[start : start + length, :].astype(jnp.bfloat16)
        full = lax.dot_general(
            left, right, (((0,), (0,)), ((), ())), preferred_element_type=jnp.float32
        )
        return jnp.where(half, full[0:32, :], full[32:64, :]) * (1.0 / length)

    damp = jnp.concatenate([eig_v[0:32, :], eig_v[32:64, :]], axis=1) + 0.1
    q2 = outer(0, 64) / damp
    t0 = outer(64, 128)
    t1 = outer(192, 128)
    for i, m in enumerate((q2, t0, t1)):
        m = m.astype(jnp.bfloat16).astype(jnp.float32)
        for kk in range(NP):
            sb1[kk, 4 * i : 4 * i + 4, :] = m[4 * kk : 4 * kk + 4, :]
    for kk in range(NP):
        sb1[kk, 12:16, :] = jnp.zeros((4, 128), jnp.float32)

    def send1(d, c):
        kk = lax.rem(k + d, NP)
        pltpu.make_async_remote_copy(
            src_ref=sb1.at[kk], dst_ref=rb1.at[k], send_sem=s1, recv_sem=r1,
            device_id=(kk * NZ + z, layer), device_id_type=MESH,
        ).start()
        return c

    lax.fori_loop(1, NP, send1, 0)
    rb1[k] = sb1[k]

    few = rb1.at[pl.ds(0, NP - 1)]
    c1 = pltpu.make_async_remote_copy(
        src_ref=few, dst_ref=few, send_sem=s1, recv_sem=r1,
        device_id=(dp, layer), device_id_type=MESH,
    )
    c1.wait_recv()

    def peers(i):
        return jnp.concatenate([rb1[p, i : i + 1, :] for p in range(NP)], axis=0)

    qb_rows = jnp.concatenate([peers(i) for i in range(4)], axis=0).astype(jnp.bfloat16)
    qa_all[z] = qb_rows

    def send2(d, c):
        pltpu.make_async_remote_copy(
            src_ref=qa_all.at[z], dst_ref=qa_all.at[z], send_sem=s2, recv_sem=r2.at[z],
            device_id=(dev(y, x, lax.rem(z + d, NZ)), layer), device_id_type=MESH,
        ).start()
        return c

    lax.fori_loop(1, NZ, send2, 0)
    train = jnp.concatenate(
        [
            jnp.concatenate([peers(4 + 4 * i + r) for i in (0, 1)], axis=0)
            for r in range(4)
        ],
        axis=1,
    ).astype(jnp.bfloat16)

    def wait2(d, c):
        zz = lax.rem(z + d, NZ)
        pltpu.make_async_remote_copy(
            src_ref=qa_all.at[zz], dst_ref=qa_all.at[zz], send_sem=s2, recv_sem=r2.at[zz],
            device_id=(dp, layer), device_id_type=MESH,
        ).wait_recv()
        return c

    lax.fori_loop(1, NZ, wait2, 0)
    every = qa_all[...].astype(jnp.float32)
    query = jnp.concatenate(
        [every[:, 8 * r : 8 * r + 8, :].reshape(64, 128) for r in range(4)], axis=1
    ).astype(jnp.bfloat16)
    part = lax.dot_general(
        train, query, (((1,), (1,)), ((), ())), preferred_element_type=jnp.float32
    )
    rows = jnp.concatenate([part[0:8, :], part[8:16, :]], axis=1)
    for kk in range(NP):
        sb3[kk] = rows[kk : kk + 1, :]

    me = k * NL + layer

    def send3(d, c):
        kk = lax.rem(k + d // NL, NP)
        ll = lax.rem(layer + lax.rem(d, NL), NL)
        pltpu.make_async_remote_copy(
            src_ref=sb3.at[kk], dst_ref=rb3.at[me], send_sem=s3, recv_sem=r3,
            device_id=(kk * NZ + z, ll), device_id_type=MESH,
        ).start()
        return c

    lax.fori_loop(1, NP * NL, send3, 0)
    rb3[me] = sb3[k]
    few3 = rb3.at[pl.ds(0, NP * NL - 1)]
    c3 = pltpu.make_async_remote_copy(
        src_ref=few3, dst_ref=few3, send_sem=s3, recv_sem=r3,
        device_id=(dp, layer), device_id_type=MESH,
    )
    c3.wait_recv()
    total = rb3[0]
    for i in range(1, NP * NL):
        total = total + rb3[i]
    lane = lax.broadcasted_iota(jnp.int32, (64, 128), 1)
    row = lax.broadcasted_iota(jnp.int32, (64, 128), 0)
    want = lax.rem(row, 8) * 8 + row // 8
    wide = jnp.broadcast_to(total, (64, 128))
    for i in (0, 1):
        out[:, i : i + 1] = jnp.sum(
            jnp.where(lane == want + 64 * i, wide, 0.0), axis=1, keepdims=True
        )

    sent = gath.at[pl.ds(0, NP * NZ - 1)]
    pltpu.make_async_remote_copy(
        src_ref=sent, dst_ref=sent, send_sem=gsend, recv_sem=r1,
        device_id=(dp, layer), device_id_type=MESH,
    ).wait_send()
    c1.wait_send()
    few2 = qa_all.at[pl.ds(0, NZ - 1)]
    pltpu.make_async_remote_copy(
        src_ref=few2, dst_ref=few2, send_sem=s2, recv_sem=r1,
        device_id=(dp, layer), device_id_type=MESH,
    ).wait_send()
    c3.wait_send()


def per_device(*args):
    any_spec = pl.BlockSpec(memory_space=pl.ANY)
    bf, f32 = jnp.bfloat16, jnp.float32
    dma = pltpu.SemaphoreType.DMA
    return pl.pallas_call(
        kernel,
        out_shape=jax.ShapeDtypeStruct((64, 2), f32),
        in_specs=[any_spec] * 7,
        out_specs=pl.BlockSpec(memory_space=pltpu.VMEM),
        scratch_shapes=[
            pltpu.VMEM((TOK, 4096), bf),
            pltpu.VMEM((TOK, 14336), bf),
            pltpu.VMEM((OUT_ROWS, 64), bf),
            pltpu.VMEM((IN_ROWS, 64), bf),
            pltpu.VMEM((64, 64), f32),
            pltpu.VMEM((NP * NZ, PACK, 128), bf),
            pltpu.VMEM((BLOCK_OUT, 128), bf),
            pltpu.VMEM((BLOCK_IN, 128), bf),
            pltpu.VMEM((TOK, 128), f32),
            pltpu.VMEM((TOK, 128), f32),
            pltpu.VMEM((NP, 16, 128), f32),
            pltpu.VMEM((NP, 16, 128), f32),
            pltpu.VMEM((NZ, 32, 128), bf),
            pltpu.VMEM((NP, 1, 128), f32),
            pltpu.VMEM((NP * NL, 1, 128), f32),
            dma((3,)),
            dma((4,)),
            dma(()),
            dma((2, NP * NZ)),
            dma(()),
            dma(()),
            dma(()),
            dma((NZ,)),
            dma(()),
            dma(()),
        ],
        compiler_params=pltpu.CompilerParams(
            collective_id=0, has_side_effects=True, vmem_limit_bytes=40 << 20
        ),
        cost_estimate=pl.CostEstimate(
            flops=2 * TOK * 18432 * 64, bytes_accessed=12 << 20, transcendentals=0
        ),
    )(*args)


def solution(mesh):
    return jax.shard_map(
        per_device,
        mesh=mesh,
        in_specs=(P("layer", "dp", None),) * 6 + (P("layer", None, None),),
        out_specs=P(None, "dp"),
        check_vma=False,
    )
```

```python
import jax
import jax.numpy as jnp
from jax import lax
from jax.experimental import pallas as pl
from jax.experimental.pallas import tpu as pltpu
from jax.sharding import PartitionSpec as P

MESH = pl.DeviceIdType.MESH
NY, NX, NZ = 4, 2, 8
NP = NY * NX
NL = 4
OUT_ROWS, IN_ROWS = 224, 64
PACK_OUT, PACK_IN = OUT_ROWS // 2, IN_ROWS // 2
PACK = PACK_OUT + PACK_IN
SPLIT = 80
PARTS = ((0, SPLIT), (SPLIT, PACK - SPLIT))
BLOCK_OUT, BLOCK_IN = OUT_ROWS * NZ, IN_ROWS * NZ
TOK_Q, TOK_T = 64, 256
TOK = TOK_Q + TOK_T


def body(
    pending, ta, tg, qa, qg, bo, bi, eig, out,
    a_in, a_out, b_o, b_i, eig_v, gath, w_out, w_in, acc_out, acc_in,
    sb1, rb1, qa_all, sb3, rb3,
    load_sem, act_sem, gsend, grecv, s1, r1, s2, r2, s3, r3,
):
    dp = lax.axis_index("dp")
    layer = lax.axis_index("layer")
    y = dp // 16
    x = lax.rem(dp // 8, 2)
    z = lax.rem(dp, 8)
    k = dp // 8
    x1 = 1 - x

    def dev(yy, xx, zz):
        return yy * 16 + xx * 8 + zz

    def ypeer(d):
        return lax.rem(y + d, NY)

    small = [
        pltpu.make_async_copy(bo.at[0], b_o, load_sem.at[0]),
        pltpu.make_async_copy(bi.at[0], b_i, load_sem.at[1]),
        pltpu.make_async_copy(eig.at[0], eig_v, load_sem.at[2]),
    ]
    for c in small:
        c.start()

    barrier = pltpu.get_barrier_semaphore()

    def greet_z(d, c):
        pl.semaphore_signal(
            barrier, inc=1, device_id=(dev(y, x, lax.rem(z + d, NZ)), layer), device_id_type=MESH
        )
        return c

    def greet_plane(d, c):
        kk = lax.rem(k + d // NL, NP)
        ll = lax.rem(layer + lax.rem(d, NL), NL)
        pl.semaphore_signal(barrier, inc=1, device_id=(kk * NZ + z, ll), device_id_type=MESH)
        return c

    lax.fori_loop(1, NZ, greet_z, 0)
    lax.fori_loop(1, NP * NL, greet_plane, 0)

    acts = [
        pltpu.make_async_copy(qa.at[0], a_in.at[pl.ds(0, TOK_Q)], act_sem.at[0]),
        pltpu.make_async_copy(ta.at[0], a_in.at[pl.ds(TOK_Q, TOK_T)], act_sem.at[1]),
        pltpu.make_async_copy(qg.at[0], a_out.at[pl.ds(0, TOK_Q)], act_sem.at[2]),
        pltpu.make_async_copy(tg.at[0], a_out.at[pl.ds(TOK_Q, TOK_T)], act_sem.at[3]),
    ]
    for c in acts:
        c.start()

    for c in small:
        c.wait()
    rows = b_o[...].astype(jnp.float32).T.astype(jnp.bfloat16)
    for t in range(PACK_OUT // 16):
        gath[dp, 16 * t : 16 * t + 16, :] = jnp.concatenate(
            [rows[32 * t : 32 * t + 16, :], rows[32 * t + 16 : 32 * t + 32, :]], axis=1
        )
    for t in range(PACK_IN // 16):
        gath[dp, PACK_OUT + 16 * t : PACK_OUT + 16 * t + 16, :] = jnp.concatenate(
            [b_i[32 * t : 32 * t + 16, :], b_i[32 * t + 16 : 32 * t + 32, :]], axis=1
        )

    pl.semaphore_wait(barrier, NZ - 1 + NP * NL - 1)

    def part_copy(j, part, to):
        start, size = PARTS[part]
        ref = gath.at[j, pl.ds(start, size)]
        return pltpu.make_async_remote_copy(
            src_ref=ref, dst_ref=ref, send_sem=gsend, recv_sem=grecv.at[part, j],
            device_id=(to, layer), device_id_type=MESH,
        )

    def arrived(j, part):
        part_copy(j, part, dp).wait_recv()

    def to_plane(j):
        for part in (0, 1):
            for d in (2, 1, 3):
                part_copy(j, part, dev(ypeer(d), x, z)).start()
            part_copy(j, part, dev(y, x1, z)).start()

    for d in (1, 7, 2, 6, 3, 5, 4):
        for part in (0, 1):
            part_copy(dp, part, dev(y, x, lax.rem(z + d, NZ))).start()
    to_plane(dp)

    def z_at(n):
        up = lax.rem(n, 2)
        off = (n + 1) // 2
        return lax.rem(z + NZ + off * (2 * up - 1), NZ)

    def first(n, c):
        j = dev(y, x, z_at(n))
        arrived(j, 0)
        arrived(j, 1)
        to_plane(j)
        return c

    def second(n, c):
        zz = z_at(n)
        j = dev(y, x1, zz)
        arrived(j, 1)
        for d in (2, 1, 3):
            part_copy(j, 1, dev(ypeer(d), x, z)).start()
        for d in (1, 3, 2):
            j = dev(ypeer(d), x, zz)
            arrived(j, 0)
            part_copy(j, 0, dev(y, x1, z)).start()
        return c

    def both(n, c):
        first(n, c)
        return second(n - 3, c)

    lax.fori_loop(1, 3, first, 0)
    lax.fori_loop(3, NZ, both, 0)
    lax.fori_loop(NZ - 3, NZ, second, 0)

    every_shard = gath.at[pl.ds(0, NP * NZ - 1)]
    pending.append(
        pltpu.make_async_remote_copy(
            src_ref=every_shard, dst_ref=every_shard, send_sem=gsend, recv_sem=grecv.at[0, 0],
            device_id=(dp, layer), device_id_type=MESH,
        ).wait_send
    )

    for c in acts:
        c.wait()
    acc_out[...] = jnp.zeros_like(acc_out)
    acc_in[...] = jnp.zeros_like(acc_in)
    low = lax.broadcasted_iota(jnp.int32, (16, 128), 1) < 64

    def block(yy, xx, parts):
        def unpack(zz, c):
            j = dev(yy, xx, zz)
            for part in parts:
                arrived(j, part)
            base = zz * OUT_ROWS
            for t in range(PACK_OUT // 16):
                tile = gath[j, 16 * t : 16 * t + 16, :]
                row = pl.multiple_of(base + 32 * t, 16)
                w_out[pl.ds(row, 16), :] = tile
                w_out[pl.ds(row + 16, 16), :] = jnp.concatenate(
                    [tile[:, 64:], tile[:, :64]], axis=1
                )
            base = zz * IN_ROWS
            for t in range(PACK_IN // 16):
                tile = gath[j, PACK_OUT + 16 * t : PACK_OUT + 16 * t + 16, :]
                row = pl.multiple_of(base + 32 * t, 16)
                turned = jnp.concatenate([tile[:, 64:], tile[:, :64]], axis=1)
                w_in[pl.ds(row, 16), :] = jnp.where(low, tile, turned)
                w_in[pl.ds(row + 16, 16), :] = jnp.where(low, turned, tile)
            return c

        lax.fori_loop(0, NZ, unpack, 0)
        kk = yy * NX + xx
        cols = pl.ds(pl.multiple_of(kk * BLOCK_IN, 128), BLOCK_IN)
        acc_in[...] += jnp.dot(a_in[:, cols], w_in[...], preferred_element_type=jnp.float32)
        cols = pl.ds(pl.multiple_of(kk * BLOCK_OUT, 128), BLOCK_OUT)
        acc_out[...] += jnp.dot(a_out[:, cols], w_out[...], preferred_element_type=jnp.float32)

    block(y, x, ())

    def same_x(d, c):
        block(ypeer(d), x, (1,))
        return c

    def other_x(d, c):
        block(ypeer(d), x1, (0, 1))
        return c

    lax.fori_loop(1, NY, same_x, 0)
    block(y, x1, (0,))
    lax.fori_loop(1, NY, other_x, 0)
    half = lax.broadcasted_iota(jnp.int32, (32, 128), 1) < 64

    def outer(start, length):
        left = acc_out[start : start + length, :].astype(jnp.bfloat16)
        right = acc_in[start : start + length, :].astype(jnp.bfloat16)
        full = lax.dot_general(
            left, right, (((0,), (0,)), ((), ())), preferred_element_type=jnp.float32
        )
        return jnp.where(half, full[0:32, :], full[32:64, :]) * (1.0 / length)

    damp = jnp.concatenate([eig_v[0:32, :], eig_v[32:64, :]], axis=1) + 0.1
    q2 = outer(0, 64) / damp
    t0 = outer(64, 128)
    t1 = outer(192, 128)
    for i, m in enumerate((q2, t0, t1)):
        m = m.astype(jnp.bfloat16).astype(jnp.float32)
        for kk in range(NP):
            sb1[kk, 4 * i : 4 * i + 4, :] = m[4 * kk : 4 * kk + 4, :]
    for kk in range(NP):
        sb1[kk, 12:16, :] = jnp.zeros((4, 128), jnp.float32)
    def send1(d, c):
        kk = lax.rem(k + d, NP)
        pltpu.make_async_remote_copy(
            src_ref=sb1.at[kk], dst_ref=rb1.at[k], send_sem=s1, recv_sem=r1,
            device_id=(kk * NZ + z, layer), device_id_type=MESH,
        ).start()
        return c

    lax.fori_loop(1, NP, send1, 0)
    rb1[k] = sb1[k]

    few = rb1.at[pl.ds(0, NP - 1)]
    c1 = pltpu.make_async_remote_copy(
        src_ref=few, dst_ref=few, send_sem=s1, recv_sem=r1,
        device_id=(dp, layer), device_id_type=MESH,
    )
    c1.wait_recv()
    pending.append(c1.wait_send)

    def peers(i):
        return jnp.concatenate([rb1[p, i : i + 1, :] for p in range(NP)], axis=0)

    qb_rows = jnp.concatenate([peers(i) for i in range(4)], axis=0).astype(jnp.bfloat16)
    qa_all[z] = qb_rows

    def send2(d, c):
        pltpu.make_async_remote_copy(
            src_ref=qa_all.at[z], dst_ref=qa_all.at[z], send_sem=s2, recv_sem=r2.at[z],
            device_id=(dev(y, x, lax.rem(z + d, NZ)), layer), device_id_type=MESH,
        ).start()
        return c

    lax.fori_loop(1, NZ, send2, 0)
    train = jnp.concatenate(
        [
            jnp.concatenate([peers(4 + 4 * i + r) for i in (0, 1)], axis=0)
            for r in range(4)
        ],
        axis=1,
    ).astype(jnp.bfloat16)

    def wait2(d, c):
        zz = lax.rem(z + d, NZ)
        pltpu.make_async_remote_copy(
            src_ref=qa_all.at[zz], dst_ref=qa_all.at[zz], send_sem=s2, recv_sem=r2.at[zz],
            device_id=(dp, layer), device_id_type=MESH,
        ).wait_recv()
        return c

    lax.fori_loop(1, NZ, wait2, 0)
    few2 = qa_all.at[pl.ds(0, NZ - 1)]
    pending.append(
        pltpu.make_async_remote_copy(
            src_ref=few2, dst_ref=few2, send_sem=s2, recv_sem=r2.at[0],
            device_id=(dp, layer), device_id_type=MESH,
        ).wait_send
    )
    every = qa_all[...].astype(jnp.float32)
    query = jnp.concatenate(
        [every[:, 8 * r : 8 * r + 8, :].reshape(64, 128) for r in range(4)], axis=1
    ).astype(jnp.bfloat16)
    part = lax.dot_general(
        train, query, (((1,), (1,)), ((), ())), preferred_element_type=jnp.float32
    )
    rows = jnp.concatenate([part[0:8, :], part[8:16, :]], axis=1)
    for kk in range(NP):
        sb3[kk] = rows[kk : kk + 1, :]
    me = k * NL + layer

    def send3(d, c):
        kk = lax.rem(k + d // NL, NP)
        ll = lax.rem(layer + lax.rem(d, NL), NL)
        pltpu.make_async_remote_copy(
            src_ref=sb3.at[kk], dst_ref=rb3.at[me], send_sem=s3, recv_sem=r3,
            device_id=(kk * NZ + z, ll), device_id_type=MESH,
        ).start()
        return c

    lax.fori_loop(1, NP * NL, send3, 0)
    rb3[me] = sb3[k]
    few3 = rb3.at[pl.ds(0, NP * NL - 1)]
    c3 = pltpu.make_async_remote_copy(
        src_ref=few3, dst_ref=few3, send_sem=s3, recv_sem=r3,
        device_id=(dp, layer), device_id_type=MESH,
    )
    c3.wait_recv()
    pending.append(c3.wait_send)
    total = rb3[0]
    for i in range(1, NP * NL):
        total = total + rb3[i]
    lane = lax.broadcasted_iota(jnp.int32, (128, 128), 1)
    row = lax.broadcasted_iota(jnp.int32, (128, 128), 0)
    half_row = lax.rem(row, 64)
    want = (row - half_row) + lax.rem(half_row, 8) * 8 + half_row // 8
    wide = jnp.broadcast_to(total, (128, 128))
    turned = jnp.sum(jnp.where(lane == want, wide, 0.0), axis=1, keepdims=True).T
    for i in (0, 1):
        out[i : i + 1, :] = turned[:, 64 * i : 64 * i + 64]


def kernel(*refs):
    pending = []
    body(pending, *refs)
    for finish in pending:
        finish()


def per_device(ta, tg, qa, qg, bo, bi, eig):
    any_spec = pl.BlockSpec(memory_space=pl.ANY)
    bf, f32 = jnp.bfloat16, jnp.float32
    dma = pltpu.SemaphoreType.DMA
    result = pl.pallas_call(
        kernel,
        out_shape=jax.ShapeDtypeStruct((2, 64), f32),
        in_specs=[any_spec] * 7,
        out_specs=pl.BlockSpec(memory_space=pltpu.VMEM),
        scratch_shapes=[
            pltpu.VMEM((TOK, 4096), bf),
            pltpu.VMEM((TOK, 14336), bf),
            pltpu.VMEM((64, OUT_ROWS), bf),
            pltpu.VMEM((IN_ROWS, 64), bf),
            pltpu.VMEM((64, 64), f32),
            pltpu.VMEM((NP * NZ, PACK, 128), bf),
            pltpu.VMEM((BLOCK_OUT, 128), bf),
            pltpu.VMEM((BLOCK_IN, 128), bf),
            pltpu.VMEM((TOK, 128), f32),
            pltpu.VMEM((TOK, 128), f32),
            pltpu.VMEM((NP, 16, 128), f32),
            pltpu.VMEM((NP, 16, 128), f32),
            pltpu.VMEM((NZ, 32, 128), bf),
            pltpu.VMEM((NP, 1, 128), f32),
            pltpu.VMEM((NP * NL, 1, 128), f32),
            dma((3,)),
            dma((4,)),
            dma(()),
            dma((2, NP * NZ)),
            dma(()),
            dma(()),
            dma(()),
            dma((NZ,)),
            dma(()),
            dma(()),
        ],
        compiler_params=pltpu.CompilerParams(
            collective_id=0, has_side_effects=True, vmem_limit_bytes=62 << 20
        ),
        cost_estimate=pl.CostEstimate(
            flops=2 * TOK * 18432 * 64, bytes_accessed=12 << 20, transcendentals=0
        ),
    )(ta, tg, qa, qg, jnp.swapaxes(bo, 1, 2), bi, eig)
    return result.T


def solution(mesh):
    return jax.shard_map(
        per_device,
        mesh=mesh,
        in_specs=(P("layer", "dp", None),) * 6 + (P("layer", None, None),),
        out_specs=P(None, "dp"),
        check_vma=False,
    )
```

```python
import jax
import jax.numpy as jnp
from jax import lax
from jax.experimental import pallas as pl
from jax.experimental.pallas import tpu as pltpu
from jax.sharding import PartitionSpec as P

MESH = pl.DeviceIdType.MESH
NY, NX, NZ = 4, 2, 8
NP = NY * NX
NL = 4
OUT_ROWS, IN_ROWS = 224, 64
PACK_OUT, PACK_IN = OUT_ROWS // 2, IN_ROWS // 2
PACK = PACK_OUT + PACK_IN
CHILDREN = {
    0: (7, 22, 19, 63, 49, 24, 1, 56, 16, 15, 8, 48),
    1: (9, 2, 17),
    4: (12,),
    5: (4, 52, 61, 13, 53),
    7: (5, 23, 55),
    9: (10,),
    16: (32,),
    19: (27, 35, 36, 3, 18, 20),
    21: (37,),
    22: (30, 29, 21, 38, 6),
    23: (31, 39),
    24: (25,),
    25: (26,),
    27: (11, 28),
    29: (45,),
    30: (44,),
    33: (34, 41),
    35: (43,),
    38: (54,),
    49: (58, 33, 50, 57),
    50: (51,),
    56: (40,),
    58: (42, 59),
    62: (60, 14, 46),
    63: (62, 47),
}
ORDER = (
    7, 1, 48, 49, 16, 22, 24, 56, 63, 8, 15, 19, 23, 55, 9, 2,
    5, 17, 33, 50, 32, 21, 57, 6, 58, 38, 30, 40, 25, 62, 47, 35,
    18, 20, -3, 27, 3, 29, 10, 31, 39, 4, -1, 36, 53, 52, 37, 34,
    -5, 13, 42, 54, 51, 41, 61, -7, 59, 60, 43, 46, 14, 26, -8, 11,
    45, 28, 12, 44, -6, -2, -4,
)
STEPS = (
    1, 2, 3, 4, 5, 6, 7, 9, 15, 17, 19, 22, 49, 55, 63,
)
BLOCK_OUT, BLOCK_IN = OUT_ROWS * NZ, IN_ROWS * NZ
TOK_Q, TOK_T = 64, 256
TOK = TOK_Q + TOK_T


def minus(a, b):
    return (
        (a // 16 - b // 16) % NY * 16 + (a // 8 + b // 8) % 2 * 8 + (a - b) % NZ
    )


def body(
    pending, ta, tg, qa, qg, bo, bi, eig, out,
    a_in, a_out, b_o, b_i, eig_v, gath, w_out, w_in, acc_out, acc_in,
    sb1, rb1, qa_all, sb3, rb3,
    load_sem, act_sem, gsend, grecv, s1, r1, s2, r2, s3, r3,
):
    dp = lax.axis_index("dp")
    layer = lax.axis_index("layer")
    y = dp // 16
    x = lax.rem(dp // 8, 2)
    z = lax.rem(dp, 8)
    k = dp // 8

    small = [
        pltpu.make_async_copy(bo.at[0], b_o, load_sem.at[0]),
        pltpu.make_async_copy(bi.at[0], b_i, load_sem.at[1]),
        pltpu.make_async_copy(eig.at[0], eig_v, load_sem.at[2]),
    ]
    for c in small:
        c.start()

    ys = [lax.rem(y + NY - d, NY) for d in range(NY)]
    xs = [x, 1 - x]
    zs = [lax.rem(z + NZ - d, NZ) for d in range(NZ)]

    def back(d):
        return ys[d // 16] * 16 + xs[d // 8 % 2] * 8 + zs[d % 8]

    def ahead(d):
        return ys[-(d // 16) % NY] * 16 + xs[d // 8 % 2] * 8 + zs[-d % NZ]

    barrier = pltpu.get_barrier_semaphore()
    for d in STEPS:
        pl.semaphore_signal(barrier, inc=1, device_id=(back(d), layer), device_id_type=MESH)

    def greet_plane(d, c):
        kk = lax.rem(k + d // NL, NP)
        ll = lax.rem(layer + lax.rem(d, NL), NL)
        pl.semaphore_signal(barrier, inc=1, device_id=(kk * NZ + z, ll), device_id_type=MESH)
        return c

    lax.fori_loop(1, NP * NL, greet_plane, 0)

    acts = [
        pltpu.make_async_copy(qa.at[0], a_in.at[pl.ds(0, TOK_Q)], act_sem.at[0]),
        pltpu.make_async_copy(ta.at[0], a_in.at[pl.ds(TOK_Q, TOK_T)], act_sem.at[1]),
        pltpu.make_async_copy(qg.at[0], a_out.at[pl.ds(0, TOK_Q)], act_sem.at[2]),
        pltpu.make_async_copy(tg.at[0], a_out.at[pl.ds(TOK_Q, TOK_T)], act_sem.at[3]),
    ]
    for c in acts:
        c.start()

    for c in small:
        c.wait()
    rows = b_o[...].astype(jnp.float32).T.astype(jnp.bfloat16)
    for t in range(PACK_OUT // 16):
        gath[dp, 16 * t : 16 * t + 16, :] = jnp.concatenate(
            [rows[32 * t : 32 * t + 16, :], rows[32 * t + 16 : 32 * t + 32, :]], axis=1
        )
    for t in range(PACK_IN // 16):
        gath[dp, PACK_OUT + 16 * t : PACK_OUT + 16 * t + 16, :] = jnp.concatenate(
            [b_i[32 * t : 32 * t + 16, :], b_i[32 * t + 16 : 32 * t + 32, :]], axis=1
        )

    pl.semaphore_wait(barrier, len(STEPS) + NP * NL - 1)

    def shard_copy(j, to):
        ref = gath.at[j]
        return pltpu.make_async_remote_copy(
            src_ref=ref, dst_ref=ref, send_sem=gsend, recv_sem=grecv.at[j],
            device_id=(to, layer), device_id_type=MESH,
        )

    low = lax.broadcasted_iota(jnp.int32, (PACK_IN, 128), 1) < 64

    def unpack(d, j):
        tile = gath[j, 0:PACK_OUT, :]
        at = pl.ds(zs[d % 8] * (PACK_OUT // 16), PACK_OUT // 16)
        w_out[d // 8, at, 0] = tile.reshape(-1, 16, 128)
        w_out[d // 8, at, 1] = pltpu.roll(tile, 64, 1).reshape(-1, 16, 128)
        tile = gath[j, PACK_OUT:PACK, :]
        turned = pltpu.roll(tile, 64, 1)
        at = pl.ds(zs[d % 8] * (PACK_IN // 16), PACK_IN // 16)
        w_in[d // 8, at, 0] = jnp.where(low, tile, turned).reshape(-1, 16, 128)
        w_in[d // 8, at, 1] = jnp.where(low, turned, tile).reshape(-1, 16, 128)

    def multiply(b, first):
        kk = ys[b // 2] * NX + xs[b % 2]
        for acts, weights, acc, rows in (
            (a_in, w_in, acc_in, BLOCK_IN), (a_out, w_out, acc_out, BLOCK_OUT),
        ):
            cols = pl.ds(pl.multiple_of(kk * rows, 128), rows)
            term = jnp.dot(
                acts[:, cols], weights[b].reshape(rows, 128), preferred_element_type=jnp.float32
            )
            acc[...] = term if first else acc[...] + term

    for child in CHILDREN[0]:
        shard_copy(dp, ahead(child)).start()
    unpack(0, dp)
    started = False
    for d in ORDER:
        if d < 0:
            if not started:
                for c in acts:
                    c.wait()
            multiply(-1 - d, not started)
            started = True
            continue
        j = back(d)
        shard_copy(j, dp).wait_recv()
        for child in CHILDREN.get(d, ()):
            shard_copy(j, ahead(minus(child, d))).start()
        unpack(d, j)

    every_shard = gath.at[pl.ds(0, NP * NZ - 1)]
    pending.append(
        pltpu.make_async_remote_copy(
            src_ref=every_shard, dst_ref=every_shard, send_sem=gsend, recv_sem=grecv.at[0],
            device_id=(dp, layer), device_id_type=MESH,
        ).wait_send
    )
    half = lax.broadcasted_iota(jnp.int32, (32, 128), 1) < 64

    def outer(start, length):
        left = acc_out[start : start + length, :].astype(jnp.bfloat16)
        right = acc_in[start : start + length, :].astype(jnp.bfloat16)
        full = lax.dot_general(
            left, right, (((0,), (0,)), ((), ())), preferred_element_type=jnp.float32
        )
        return jnp.where(half, full[0:32, :], full[32:64, :]) * (1.0 / length)

    damp = jnp.concatenate([eig_v[0:32, :], eig_v[32:64, :]], axis=1) + 0.1
    q2 = outer(0, 64) / damp
    t0 = outer(64, 128)
    t1 = outer(192, 128)
    for i, m in enumerate((q2, t0, t1)):
        m = m.astype(jnp.bfloat16).astype(jnp.float32)
        for kk in range(NP):
            sb1[kk, 4 * i : 4 * i + 4, :] = m[4 * kk : 4 * kk + 4, :]
    for kk in range(NP):
        sb1[kk, 12:16, :] = jnp.zeros((4, 128), jnp.float32)
    def send1(d, c):
        kk = lax.rem(k + d, NP)
        pltpu.make_async_remote_copy(
            src_ref=sb1.at[kk], dst_ref=rb1.at[k], send_sem=s1, recv_sem=r1,
            device_id=(kk * NZ + z, layer), device_id_type=MESH,
        ).start()
        return c

    lax.fori_loop(1, NP, send1, 0)
    rb1[k] = sb1[k]

    few = rb1.at[pl.ds(0, NP - 1)]
    c1 = pltpu.make_async_remote_copy(
        src_ref=few, dst_ref=few, send_sem=s1, recv_sem=r1,
        device_id=(dp, layer), device_id_type=MESH,
    )
    c1.wait_recv()
    pending.append(c1.wait_send)

    def peers(i):
        return jnp.concatenate([rb1[p, i : i + 1, :] for p in range(NP)], axis=0)

    qb_rows = jnp.concatenate([peers(i) for i in range(4)], axis=0).astype(jnp.bfloat16)
    qa_all[z] = qb_rows

    def send2(d, c):
        pltpu.make_async_remote_copy(
            src_ref=qa_all.at[z], dst_ref=qa_all.at[z], send_sem=s2, recv_sem=r2.at[z],
            device_id=(k * NZ + lax.rem(z + d, NZ), layer), device_id_type=MESH,
        ).start()
        return c

    lax.fori_loop(1, NZ, send2, 0)
    train = jnp.concatenate(
        [
            jnp.concatenate([peers(4 + 4 * i + r) for i in (0, 1)], axis=0)
            for r in range(4)
        ],
        axis=1,
    ).astype(jnp.bfloat16)

    def wait2(d, c):
        zz = lax.rem(z + d, NZ)
        pltpu.make_async_remote_copy(
            src_ref=qa_all.at[zz], dst_ref=qa_all.at[zz], send_sem=s2, recv_sem=r2.at[zz],
            device_id=(dp, layer), device_id_type=MESH,
        ).wait_recv()
        return c

    lax.fori_loop(1, NZ, wait2, 0)
    few2 = qa_all.at[pl.ds(0, NZ - 1)]
    pending.append(
        pltpu.make_async_remote_copy(
            src_ref=few2, dst_ref=few2, send_sem=s2, recv_sem=r2.at[0],
            device_id=(dp, layer), device_id_type=MESH,
        ).wait_send
    )
    every = qa_all[...].astype(jnp.float32)
    query = jnp.concatenate(
        [every[:, 8 * r : 8 * r + 8, :].reshape(64, 128) for r in range(4)], axis=1
    ).astype(jnp.bfloat16)
    part = lax.dot_general(
        train, query, (((1,), (1,)), ((), ())), preferred_element_type=jnp.float32
    )
    rows = jnp.concatenate([part[0:8, :], part[8:16, :]], axis=1)
    for kk in range(NP):
        sb3[kk] = rows[kk : kk + 1, :]
    me = k * NL + layer

    def send3(d, c):
        kk = lax.rem(k + d // NL, NP)
        ll = lax.rem(layer + lax.rem(d, NL), NL)
        pltpu.make_async_remote_copy(
            src_ref=sb3.at[kk], dst_ref=rb3.at[me], send_sem=s3, recv_sem=r3,
            device_id=(kk * NZ + z, ll), device_id_type=MESH,
        ).start()
        return c

    lax.fori_loop(1, NP * NL, send3, 0)
    rb3[me] = sb3[k]
    few3 = rb3.at[pl.ds(0, NP * NL - 1)]
    c3 = pltpu.make_async_remote_copy(
        src_ref=few3, dst_ref=few3, send_sem=s3, recv_sem=r3,
        device_id=(dp, layer), device_id_type=MESH,
    )
    c3.wait_recv()
    pending.append(c3.wait_send)
    total = rb3[0]
    for i in range(1, NP * NL):
        total = total + rb3[i]
    lane = lax.broadcasted_iota(jnp.int32, (128, 128), 1)
    row = lax.broadcasted_iota(jnp.int32, (128, 128), 0)
    half_row = lax.rem(row, 64)
    want = (row - half_row) + lax.rem(half_row, 8) * 8 + half_row // 8
    wide = jnp.broadcast_to(total, (128, 128))
    turned = jnp.sum(jnp.where(lane == want, wide, 0.0), axis=1, keepdims=True).T
    for i in (0, 1):
        out[i : i + 1, :] = turned[:, 64 * i : 64 * i + 64]


def kernel(*refs):
    pending = []
    body(pending, *refs)
    for finish in pending:
        finish()


def per_device(ta, tg, qa, qg, bo, bi, eig):
    any_spec = pl.BlockSpec(memory_space=pl.ANY)
    bf, f32 = jnp.bfloat16, jnp.float32
    dma = pltpu.SemaphoreType.DMA
    result = pl.pallas_call(
        kernel,
        out_shape=jax.ShapeDtypeStruct((2, 64), f32),
        in_specs=[any_spec] * 7,
        out_specs=pl.BlockSpec(memory_space=pltpu.VMEM),
        scratch_shapes=[
            pltpu.VMEM((TOK, 4096), bf),
            pltpu.VMEM((TOK, 14336), bf),
            pltpu.VMEM((64, OUT_ROWS), bf),
            pltpu.VMEM((IN_ROWS, 64), bf),
            pltpu.VMEM((64, 64), f32),
            pltpu.VMEM((NP * NZ, PACK, 128), bf),
            pltpu.VMEM((NP, BLOCK_OUT // 32, 2, 16, 128), bf),
            pltpu.VMEM((NP, BLOCK_IN // 32, 2, 16, 128), bf),
            pltpu.VMEM((TOK, 128), f32),
            pltpu.VMEM((TOK, 128), f32),
            pltpu.VMEM((NP, 16, 128), f32),
            pltpu.VMEM((NP, 16, 128), f32),
            pltpu.VMEM((NZ, 32, 128), bf),
            pltpu.VMEM((NP, 1, 128), f32),
            pltpu.VMEM((NP * NL, 1, 128), f32),
            dma((3,)),
            dma((4,)),
            dma(()),
            dma((NP * NZ,)),
            dma(()),
            dma(()),
            dma(()),
            dma((NZ,)),
            dma(()),
            dma(()),
        ],
        compiler_params=pltpu.CompilerParams(
            collective_id=0, has_side_effects=True, vmem_limit_bytes=62 << 20
        ),
        cost_estimate=pl.CostEstimate(
            flops=2 * TOK * 18432 * 64, bytes_accessed=12 << 20, transcendentals=0
        ),
    )(ta, tg, qa, qg, jnp.swapaxes(bo, 1, 2), bi, eig)
    return result.T


def solution(mesh):
    return jax.shard_map(
        per_device,
        mesh=mesh,
        in_specs=(P("layer", "dp", None),) * 6 + (P("layer", None, None),),
        out_specs=P(None, "dp"),
        check_vma=False,
    )
```

```python
import jax
import jax.numpy as jnp
from jax import lax
from jax.experimental import pallas as pl
from jax.experimental.pallas import tpu as pltpu
from jax.sharding import PartitionSpec as P

MESH = pl.DeviceIdType.MESH
NY, NX, NZ = 4, 2, 8
NP = NY * NX
NL = 4
OUT_ROWS, IN_ROWS = 224, 64
PACK_OUT, PACK_IN = OUT_ROWS // 2, IN_ROWS // 2
PACK = PACK_OUT + PACK_IN
CHILDREN = {
    0: (3, 6, 48, 40, 24, 1, 8, 16),
    1: (2, 17, 9),
    2: (10,),
    3: (19, 59, 11, 51),
    5: (21, 53, 4, 13),
    6: (62, 5, 22, 54),
    8: (15,),
    11: (12, 27),
    15: (14,),
    17: (18, 33),
    19: (20,),
    20: (28, 36),
    21: (29, 37),
    24: (25, 31),
    25: (41,),
    31: (23, 30),
    39: (38,),
    40: (42, 47),
    42: (44, 26, 34, 58),
    46: (45,),
    48: (55, 49, 56, 32),
    49: (50, 57),
    51: (35,),
    53: (52,),
    55: (39, 7),
    56: (63,),
    59: (43, 60),
    62: (46, 61),
}
ORDER = (
    48, 16, 6, 1, 8, 24, 40, 3, 55, 49, 56, 32, 5, 54, 2, 22,
    17, 9, 15, 62, 25, 19, 31, 51, 47, 11, 7, 59, 42, 63, 50, 39,
    21, 57, 4, -1, 53, 18, 33, 13, 10, 46, 41, 20, 14, 23, 61, 35,
    -3, 27, 30, 12, -2, 34, 58, 43, 38, 26, 29, 37, 60, -8, 52, 44,
    -7, 28, 36, 45, -6, -5, -4,
)
STEPS = (
    1, 2, 3, 4, 5, 6, 7,
)
BLOCK_OUT, BLOCK_IN = OUT_ROWS * NZ, IN_ROWS * NZ
TOK_Q, TOK_T = 64, 256
TOK = TOK_Q + TOK_T


def minus(a, b):
    return (
        (a // 16 - b // 16) % NY * 16 + (a // 8 + b // 8) % 2 * 8 + (a - b) % NZ
    )


def body(
    pending, ta, tg, qa, qg, bo, bi, eig, out,
    a_in, a_out, b_o, b_i, eig_v, gath, w_out, w_in, acc_out, acc_in,
    sq, rq, st, rt, sb3, rb3,
    load_sem, act_sem, gsend, grecv, s1, r1, s2, r2, s3, r3,
):
    dp = lax.axis_index("dp")
    layer = lax.axis_index("layer")
    y = dp // 16
    x = lax.rem(dp // 8, 2)
    z = lax.rem(dp, 8)
    k = dp // 8

    small = [
        pltpu.make_async_copy(bo.at[0], b_o, load_sem.at[0]),
        pltpu.make_async_copy(bi.at[0], b_i, load_sem.at[1]),
        pltpu.make_async_copy(eig.at[0], eig_v, load_sem.at[2]),
    ]
    for c in small:
        c.start()

    ys = [lax.rem(y + NY - d, NY) for d in range(NY)]
    xs = [x, 1 - x]
    zs = [lax.rem(z + NZ - d, NZ) for d in range(NZ)]

    def back(d):
        return ys[d // 16] * 16 + xs[d // 8 % 2] * 8 + zs[d % 8]

    def ahead(d):
        return ys[-(d // 16) % NY] * 16 + xs[d // 8 % 2] * 8 + zs[-d % NZ]

    barrier = pltpu.get_barrier_semaphore()
    for d in STEPS:
        pl.semaphore_signal(barrier, inc=1, device_id=(back(d), layer), device_id_type=MESH)

    def greet_plane(d, c):
        kk = lax.rem(k + d // NL, NP)
        ll = lax.rem(layer + lax.rem(d, NL), NL)
        pl.semaphore_signal(barrier, inc=1, device_id=(kk * NZ + z, ll), device_id_type=MESH)
        return c

    lax.fori_loop(1, NP * NL, greet_plane, 0)

    acts = [
        pltpu.make_async_copy(qa.at[0], a_in.at[pl.ds(0, TOK_Q)], act_sem.at[0]),
        pltpu.make_async_copy(ta.at[0], a_in.at[pl.ds(TOK_Q, TOK_T)], act_sem.at[1]),
        pltpu.make_async_copy(qg.at[0], a_out.at[pl.ds(0, TOK_Q)], act_sem.at[2]),
        pltpu.make_async_copy(tg.at[0], a_out.at[pl.ds(TOK_Q, TOK_T)], act_sem.at[3]),
    ]
    for c in acts:
        c.start()

    for c in small:
        c.wait()
    sb3[...] = jnp.zeros_like(sb3)
    rows = b_o[...].astype(jnp.float32).T.astype(jnp.bfloat16)
    for t in range(PACK_OUT // 16):
        gath[dp, 16 * t : 16 * t + 16, :] = jnp.concatenate(
            [rows[32 * t : 32 * t + 16, :], rows[32 * t + 16 : 32 * t + 32, :]], axis=1
        )
    for t in range(PACK_IN // 16):
        gath[dp, PACK_OUT + 16 * t : PACK_OUT + 16 * t + 16, :] = jnp.concatenate(
            [b_i[32 * t : 32 * t + 16, :], b_i[32 * t + 16 : 32 * t + 32, :]], axis=1
        )

    pl.semaphore_wait(barrier, len(STEPS) + NP * NL - 1)

    def shard_copy(j, to):
        ref = gath.at[j]
        return pltpu.make_async_remote_copy(
            src_ref=ref, dst_ref=ref, send_sem=gsend, recv_sem=grecv.at[j],
            device_id=(to, layer), device_id_type=MESH,
        )

    low = lax.broadcasted_iota(jnp.int32, (PACK_IN, 128), 1) < 64

    def unpack(d, j):
        tile = gath[j, 0:PACK_OUT, :]
        at = pl.ds(zs[d % 8] * (PACK_OUT // 16), PACK_OUT // 16)
        w_out[d // 8, at, 0] = tile.reshape(-1, 16, 128)
        w_out[d // 8, at, 1] = pltpu.roll(tile, 64, 1).reshape(-1, 16, 128)
        tile = gath[j, PACK_OUT:PACK, :]
        turned = pltpu.roll(tile, 64, 1)
        at = pl.ds(zs[d % 8] * (PACK_IN // 16), PACK_IN // 16)
        w_in[d // 8, at, 0] = jnp.where(low, tile, turned).reshape(-1, 16, 128)
        w_in[d // 8, at, 1] = jnp.where(low, turned, tile).reshape(-1, 16, 128)

    def multiply(b, first, tokens):
        kk = ys[b // 2] * NX + xs[b % 2]
        for acts, weights, acc, rows in (
            (a_in, w_in, acc_in, BLOCK_IN), (a_out, w_out, acc_out, BLOCK_OUT),
        ):
            cols = pl.ds(pl.multiple_of(kk * rows, 128), rows)
            term = jnp.dot(
                acts[tokens, cols], weights[b].reshape(rows, 128),
                preferred_element_type=jnp.float32,
            )
            acc[tokens, :] = term if first else acc[tokens, :] + term

    queries, trains = slice(0, TOK_Q), slice(TOK_Q, TOK)
    for child in CHILDREN[0]:
        shard_copy(dp, ahead(child)).start()
    unpack(0, dp)
    started = False
    for d in ORDER[:-1]:
        if d < 0:
            if not started:
                for c in acts:
                    c.wait()
            multiply(-1 - d, not started, slice(0, TOK))
            started = True
            continue
        j = back(d)
        shard_copy(j, dp).wait_recv()
        for child in CHILDREN.get(d, ()):
            shard_copy(j, ahead(minus(child, d))).start()
        unpack(d, j)

    every_shard = gath.at[pl.ds(0, NP * NZ - 1)]
    pending.append(
        pltpu.make_async_remote_copy(
            src_ref=every_shard, dst_ref=every_shard, send_sem=gsend, recv_sem=grecv.at[0],
            device_id=(dp, layer), device_id_type=MESH,
        ).wait_send
    )
    half = lax.broadcasted_iota(jnp.int32, (32, 128), 1) < 64

    def outer(start, length):
        left = acc_out[start : start + length, :].astype(jnp.bfloat16)
        right = acc_in[start : start + length, :].astype(jnp.bfloat16)
        full = lax.dot_general(
            left, right, (((0,), (0,)), ((), ())), preferred_element_type=jnp.float32
        )
        return jnp.where(half, full[0:32, :], full[32:64, :]) * (1.0 / length)

    def rounded(m):
        return m.astype(jnp.bfloat16).astype(jnp.float32).reshape(4, NP, 128)

    def entries(d, kk):
        return pltpu.make_async_remote_copy(
            src_ref=sq.at[:, kk, :], dst_ref=rq.at[:, dp, :], send_sem=s1, recv_sem=r1,
            device_id=(d, layer), device_id_type=MESH,
        )

    def train_entries(kk):
        return pltpu.make_async_remote_copy(
            src_ref=st.at[:, kk, :], dst_ref=rt.at[:, k, :], send_sem=s2, recv_sem=r2,
            device_id=(kk * NZ + z, layer), device_id_type=MESH,
        )

    damp = jnp.concatenate([eig_v[0:32, :], eig_v[32:64, :]], axis=1) + 0.1
    multiply(-1 - ORDER[-1], False, queries)
    sq[...] = rounded(outer(0, 64) / damp)
    own_q = pltpu.make_async_copy(sq.at[:, k, :], rq.at[:, dp, :], load_sem.at[0])
    own_q.start()

    for dz in (4, 3, 5, 2, 6, 1, 7, 0):
        def send(n, c, dz=dz):
            kk = lax.rem(k + NP - n, NP)
            entries(kk * NZ + lax.rem(z + dz, NZ), kk).start()
            return c

        lax.fori_loop(1 if dz == 0 else 0, NP, send, 0)

    multiply(-1 - ORDER[-1], False, trains)
    st[0:4] = rounded(outer(64, 128))
    st[4:8] = rounded(outer(192, 128))
    own_t = pltpu.make_async_copy(st.at[:, k, :], rt.at[:, k, :], load_sem.at[1])
    own_t.start()

    def send_train(n, c):
        train_entries(lax.rem(k + n, NP)).start()
        return c

    lax.fori_loop(1, NP, send_train, 0)
    own_q.wait()
    own_t.wait()

    def whole(ref, send, recv):
        return pltpu.make_async_remote_copy(
            src_ref=ref, dst_ref=ref, send_sem=send, recv_sem=recv,
            device_id=(dp, layer), device_id_type=MESH,
        )

    some_t = whole(rt.at[:, pl.ds(0, NP - 1), :], s2, r2)
    some_t.wait_recv()
    train = jnp.concatenate(
        [jnp.concatenate([rt[r], rt[4 + r]], axis=0) for r in range(4)], axis=1
    ).astype(jnp.bfloat16)
    some_q = whole(rq.at[:, pl.ds(0, NP * NZ - 1), :], s1, r1)
    some_q.wait_recv()
    pending.append(some_q.wait_send)
    pending.append(some_t.wait_send)
    query = jnp.concatenate([rq[r] for r in range(4)], axis=1).astype(jnp.bfloat16)
    part = lax.dot_general(
        train, query, (((1,), (1,)), ((), ())), preferred_element_type=jnp.float32
    )
    sb3[:, :, 0:64] = part.reshape(2, NP, 64)
    me = k * NL + layer

    def send3(d, c):
        kk = lax.rem(k + d // NL, NP)
        ll = lax.rem(layer + lax.rem(d, NL), NL)
        pltpu.make_async_remote_copy(
            src_ref=sb3.at[:, kk, :], dst_ref=rb3.at[:, me, :], send_sem=s3, recv_sem=r3,
            device_id=(kk * NZ + z, ll), device_id_type=MESH,
        ).start()
        return c

    lax.fori_loop(1, NP * NL, send3, 0)
    own = pltpu.make_async_copy(sb3.at[:, k, :], rb3.at[:, me, :], load_sem.at[2])
    own.start()
    own.wait()
    some = whole(rb3.at[:, pl.ds(0, NP * NL - 1), :], s3, r3)
    some.wait_recv()
    pending.append(some.wait_send)
    out[...] = jnp.sum(rb3[...], axis=1)[:, 0:64]


def kernel(*refs):
    pending = []
    body(pending, *refs)
    for finish in pending:
        finish()


def per_device(ta, tg, qa, qg, bo, bi, eig):
    any_spec = pl.BlockSpec(memory_space=pl.ANY)
    bf, f32 = jnp.bfloat16, jnp.float32
    dma = pltpu.SemaphoreType.DMA
    result = pl.pallas_call(
        kernel,
        out_shape=jax.ShapeDtypeStruct((2, 64), f32),
        in_specs=[any_spec] * 7,
        out_specs=pl.BlockSpec(memory_space=pltpu.VMEM),
        scratch_shapes=[
            pltpu.VMEM((TOK, 4096), bf),
            pltpu.VMEM((TOK, 14336), bf),
            pltpu.VMEM((64, OUT_ROWS), bf),
            pltpu.VMEM((IN_ROWS, 64), bf),
            pltpu.VMEM((64, 64), f32),
            pltpu.VMEM((NP * NZ, PACK, 128), bf),
            pltpu.VMEM((NP, BLOCK_OUT // 32, 2, 16, 128), bf),
            pltpu.VMEM((NP, BLOCK_IN // 32, 2, 16, 128), bf),
            pltpu.VMEM((TOK, 128), f32),
            pltpu.VMEM((TOK, 128), f32),
            pltpu.VMEM((4, NP, 128), f32),
            pltpu.VMEM((4, NP * NZ, 128), f32),
            pltpu.VMEM((8, NP, 128), f32),
            pltpu.VMEM((8, NP, 128), f32),
            pltpu.VMEM((2, NP, 128), f32),
            pltpu.VMEM((2, NP * NL, 128), f32),
            dma((3,)),
            dma((4,)),
            dma(()),
            dma((NP * NZ,)),
            dma(()),
            dma(()),
            dma(()),
            dma(()),
            dma(()),
            dma(()),
        ],
        compiler_params=pltpu.CompilerParams(
            collective_id=0, has_side_effects=True, vmem_limit_bytes=62 << 20
        ),
        cost_estimate=pl.CostEstimate(
            flops=2 * TOK * 18432 * 64, bytes_accessed=12 << 20, transcendentals=0
        ),
    )(ta, tg, qa, qg, jnp.swapaxes(bo, 1, 2), bi, eig)
    return result.T


def solution(mesh):
    return jax.shard_map(
        per_device,
        mesh=mesh,
        in_specs=(P("layer", "dp", None),) * 6 + (P("layer", None, None),),
        out_specs=P(None, "dp"),
        check_vma=False,
    )
```

```python
import jax
import jax.numpy as jnp
from jax import lax
from jax.experimental import pallas as pl
from jax.experimental.pallas import tpu as pltpu
from jax.sharding import PartitionSpec as P

MESH = pl.DeviceIdType.MESH
NY, NX, NZ = 4, 2, 8
NP = NY * NX
NL = 4
OUT_ROWS, IN_ROWS = 224, 64
PACK_OUT, PACK_IN = OUT_ROWS // 2, IN_ROWS // 2
PACK = PACK_OUT + PACK_IN
CHILDREN = {
    0: (5, 16, 48, 40, 3, 2, 8),
    2: (50, 1, 10, 18),
    3: (11, 19, 51),
    4: (52, 20),
    5: (4, 53, 29, 6, 13, 21),
    6: (14,),
    7: (15,),
    8: (9, 56),
    9: (25, 57),
    11: (27, 59),
    13: (12,),
    16: (23, 24, 32, 17),
    19: (35,),
    21: (22, 37),
    23: (7, 39, 31),
    24: (26,),
    29: (28, 30, 45),
    32: (33,),
    39: (47,),
    40: (46, 41),
    41: (43, 42),
    46: (44,),
    48: (55, 49),
    50: (34, 58),
    52: (36,),
    53: (61,),
    54: (38, 62),
    55: (54,),
    56: (63,),
    61: (60,),
}
ORDER = (
    16, 48, 8, 5, 40, 2, 3, 24, 32, 23, 55, 56, 17, 53, 21, 49,
    4, 13, 9, 50, 29, 6, 51, 18, 46, 10, 41, 1, 11, 19, 7, -1,
    31, 39, 54, 63, 61, 52, 33, -7, 37, 26, 12, 57, 58, 20, 22, -3,
    34, 14, 28, 25, 59, 30, 15, -2, 45, 44, 38, 27, 42, 60, 35, 47,
    36, 62, 43, -6, -8, -5, -4,
)
LATE = 4
STEPS = (
    1, 2, 3, 4, 5, 6, 7,
)
BLOCK_OUT, BLOCK_IN = OUT_ROWS * NZ, IN_ROWS * NZ
TOK_Q, TOK_T = 64, 256
TOK = TOK_Q + TOK_T


def minus(a, b):
    return (
        (a // 16 - b // 16) % NY * 16 + (a // 8 + b // 8) % 2 * 8 + (a - b) % NZ
    )


def body(
    pending, ta, tg, qa, qg, bo, bi, eig, out,
    a_in, a_out, b_o, b_i, eig_v, gath, w_out, w_in, acc_out, acc_in,
    sq, rq, st, rt, sb3, rb3,
    load_sem, act_sem, gsend, grecv, s1, r1, s2, r2, s3, r3,
):
    dp = lax.axis_index("dp")
    layer = lax.axis_index("layer")
    y = dp // 16
    x = lax.rem(dp // 8, 2)
    z = lax.rem(dp, 8)
    k = dp // 8

    small = [
        pltpu.make_async_copy(bo.at[0], b_o, load_sem.at[0]),
        pltpu.make_async_copy(bi.at[0], b_i, load_sem.at[1]),
        pltpu.make_async_copy(eig.at[0], eig_v, load_sem.at[2]),
    ]
    for c in small:
        c.start()

    ys = [lax.rem(y + NY - d, NY) for d in range(NY)]
    xs = [x, 1 - x]
    zs = [lax.rem(z + NZ - d, NZ) for d in range(NZ)]

    def back(d):
        return ys[d // 16] * 16 + xs[d // 8 % 2] * 8 + zs[d % 8]

    def ahead(d):
        return ys[-(d // 16) % NY] * 16 + xs[d // 8 % 2] * 8 + zs[-d % NZ]

    barrier = pltpu.get_barrier_semaphore()
    for d in STEPS:
        pl.semaphore_signal(barrier, inc=1, device_id=(back(d), layer), device_id_type=MESH)

    def greet_plane(d, c):
        kk = lax.rem(k + d // NL, NP)
        ll = lax.rem(layer + lax.rem(d, NL), NL)
        pl.semaphore_signal(barrier, inc=1, device_id=(kk * NZ + z, ll), device_id_type=MESH)
        return c

    lax.fori_loop(1, NP * NL, greet_plane, 0)

    acts = [
        pltpu.make_async_copy(qa.at[0], a_in.at[pl.ds(0, TOK_Q)], act_sem.at[0]),
        pltpu.make_async_copy(ta.at[0], a_in.at[pl.ds(TOK_Q, TOK_T)], act_sem.at[1]),
        pltpu.make_async_copy(qg.at[0], a_out.at[pl.ds(0, TOK_Q)], act_sem.at[2]),
        pltpu.make_async_copy(tg.at[0], a_out.at[pl.ds(TOK_Q, TOK_T)], act_sem.at[3]),
    ]
    for c in acts:
        c.start()

    for c in small:
        c.wait()
    sb3[...] = jnp.zeros_like(sb3)
    rows = b_o[...].astype(jnp.float32).T.astype(jnp.bfloat16)
    for t in range(PACK_OUT // 16):
        gath[dp, 16 * t : 16 * t + 16, :] = jnp.concatenate(
            [rows[32 * t : 32 * t + 16, :], rows[32 * t + 16 : 32 * t + 32, :]], axis=1
        )
    for t in range(PACK_IN // 16):
        gath[dp, PACK_OUT + 16 * t : PACK_OUT + 16 * t + 16, :] = jnp.concatenate(
            [b_i[32 * t : 32 * t + 16, :], b_i[32 * t + 16 : 32 * t + 32, :]], axis=1
        )

    pl.semaphore_wait(barrier, len(STEPS) + NP * NL - 1)

    def shard_copy(j, to):
        ref = gath.at[j]
        return pltpu.make_async_remote_copy(
            src_ref=ref, dst_ref=ref, send_sem=gsend, recv_sem=grecv.at[j],
            device_id=(to, layer), device_id_type=MESH,
        )

    low = lax.broadcasted_iota(jnp.int32, (PACK_IN, 128), 1) < 64

    def unpack(d, j):
        tile = gath[j, 0:PACK_OUT, :]
        at = pl.ds(zs[d % 8] * (PACK_OUT // 16), PACK_OUT // 16)
        w_out[d // 8, at, 0] = tile.reshape(-1, 16, 128)
        w_out[d // 8, at, 1] = pltpu.roll(tile, 64, 1).reshape(-1, 16, 128)
        tile = gath[j, PACK_OUT:PACK, :]
        turned = pltpu.roll(tile, 64, 1)
        at = pl.ds(zs[d % 8] * (PACK_IN // 16), PACK_IN // 16)
        w_in[d // 8, at, 0] = jnp.where(low, tile, turned).reshape(-1, 16, 128)
        w_in[d // 8, at, 1] = jnp.where(low, turned, tile).reshape(-1, 16, 128)

    def multiply(b, first, tokens):
        kk = ys[b // 2] * NX + xs[b % 2]
        for acts, weights, acc, rows in (
            (a_in, w_in, acc_in, BLOCK_IN), (a_out, w_out, acc_out, BLOCK_OUT),
        ):
            cols = pl.ds(pl.multiple_of(kk * rows, 128), rows)
            term = jnp.dot(
                acts[tokens, cols], weights[b].reshape(rows, 128),
                preferred_element_type=jnp.float32,
            )
            acc[tokens, :] = term if first else acc[tokens, :] + term

    queries, trains = slice(0, TOK_Q), slice(TOK_Q, TOK)
    for child in CHILDREN[0]:
        shard_copy(dp, ahead(child)).start()
    unpack(0, dp)
    started = False
    for d in ORDER[: len(ORDER) - LATE]:
        if d < 0:
            if not started:
                for c in acts:
                    c.wait()
            multiply(-1 - d, not started, slice(0, TOK))
            started = True
            continue
        j = back(d)
        shard_copy(j, dp).wait_recv()
        for child in CHILDREN.get(d, ()):
            shard_copy(j, ahead(minus(child, d))).start()
        unpack(d, j)

    every_shard = gath.at[pl.ds(0, NP * NZ - 1)]
    pending.append(
        pltpu.make_async_remote_copy(
            src_ref=every_shard, dst_ref=every_shard, send_sem=gsend, recv_sem=grecv.at[0],
            device_id=(dp, layer), device_id_type=MESH,
        ).wait_send
    )
    half = lax.broadcasted_iota(jnp.int32, (32, 128), 1) < 64

    def outer(start, length):
        left = acc_out[start : start + length, :].astype(jnp.bfloat16)
        right = acc_in[start : start + length, :].astype(jnp.bfloat16)
        full = lax.dot_general(
            left, right, (((0,), (0,)), ((), ())), preferred_element_type=jnp.float32
        )
        return jnp.where(half, full[0:32, :], full[32:64, :]) * (1.0 / length)

    def rounded(m):
        return m.astype(jnp.bfloat16).astype(jnp.float32).reshape(4, NP, 128)

    def entries(d, kk):
        return pltpu.make_async_remote_copy(
            src_ref=sq.at[:, kk, :], dst_ref=rq.at[:, dp, :], send_sem=s1, recv_sem=r1,
            device_id=(d, layer), device_id_type=MESH,
        )

    def train_entries(kk):
        return pltpu.make_async_remote_copy(
            src_ref=st.at[:, kk, :], dst_ref=rt.at[:, k, :], send_sem=s2, recv_sem=r2,
            device_id=(kk * NZ + z, layer), device_id_type=MESH,
        )

    damp = jnp.concatenate([eig_v[0:32, :], eig_v[32:64, :]], axis=1) + 0.1
    late = [-1 - d for d in ORDER[len(ORDER) - LATE :]]
    for b in late:
        multiply(b, False, queries)
    sq[...] = rounded(outer(0, 64) / damp)
    own_q = pltpu.make_async_copy(sq.at[:, k, :], rq.at[:, dp, :], load_sem.at[0])
    own_q.start()

    for dz in (4, 3, 5, 2, 6, 1, 7, 0):
        def send(n, c, dz=dz):
            kk = lax.rem(k + NP - n, NP)
            entries(kk * NZ + lax.rem(z + dz, NZ), kk).start()
            return c

        lax.fori_loop(1 if dz == 0 else 0, NP, send, 0)

    for b in late:
        multiply(b, False, trains)
    st[0:4] = rounded(outer(64, 128))
    st[4:8] = rounded(outer(192, 128))
    own_t = pltpu.make_async_copy(st.at[:, k, :], rt.at[:, k, :], load_sem.at[1])
    own_t.start()

    def send_train(n, c):
        train_entries(lax.rem(k + n, NP)).start()
        return c

    lax.fori_loop(1, NP, send_train, 0)
    own_q.wait()
    own_t.wait()

    def whole(ref, send, recv):
        return pltpu.make_async_remote_copy(
            src_ref=ref, dst_ref=ref, send_sem=send, recv_sem=recv,
            device_id=(dp, layer), device_id_type=MESH,
        )

    some_t = whole(rt.at[:, pl.ds(0, NP - 1), :], s2, r2)
    some_t.wait_recv()
    train = jnp.concatenate(
        [jnp.concatenate([rt[r], rt[4 + r]], axis=0) for r in range(4)], axis=1
    ).astype(jnp.bfloat16)
    some_q = whole(rq.at[:, pl.ds(0, NP * NZ - 1), :], s1, r1)
    some_q.wait_recv()
    pending.append(some_q.wait_send)
    pending.append(some_t.wait_send)
    query = jnp.concatenate([rq[r] for r in range(4)], axis=1).astype(jnp.bfloat16)
    part = lax.dot_general(
        train, query, (((1,), (1,)), ((), ())), preferred_element_type=jnp.float32
    )
    sb3[:, :, 0:64] = part.reshape(2, NP, 64)
    me = k * NL + layer

    own = pltpu.make_async_copy(sb3.at[:, k, :], rb3.at[:, me, :], load_sem.at[2])
    for dk in (4, 5, 2, 6, 3, 7, 1, 0):
        for dl in (2, 3, 1, 0):
            if dk or dl:
                kk = lax.rem(k + dk, NP)
                ll = lax.rem(layer + dl, NL)
                pltpu.make_async_remote_copy(
                    src_ref=sb3.at[:, kk, :], dst_ref=rb3.at[:, me, :], send_sem=s3, recv_sem=r3,
                    device_id=(kk * NZ + z, ll), device_id_type=MESH,
                ).start()
    own.start()
    own.wait()
    some = whole(rb3.at[:, pl.ds(0, NP * NL - 1), :], s3, r3)
    some.wait_recv()
    pending.append(some.wait_send)
    out[...] = jnp.sum(rb3[...], axis=1)[:, 0:64]


def kernel(*refs):
    pending = []
    body(pending, *refs)
    for finish in pending:
        finish()


def per_device(ta, tg, qa, qg, bo, bi, eig):
    any_spec = pl.BlockSpec(memory_space=pl.ANY)
    bf, f32 = jnp.bfloat16, jnp.float32
    dma = pltpu.SemaphoreType.DMA
    result = pl.pallas_call(
        kernel,
        out_shape=pltpu.VMEM((2, 64), f32),
        in_specs=[any_spec] * 7,
        out_specs=pl.BlockSpec(memory_space=pltpu.VMEM),
        scratch_shapes=[
            pltpu.VMEM((TOK, 4096), bf),
            pltpu.VMEM((TOK, 14336), bf),
            pltpu.VMEM((64, OUT_ROWS), bf),
            pltpu.VMEM((IN_ROWS, 64), bf),
            pltpu.VMEM((64, 64), f32),
            pltpu.VMEM((NP * NZ, PACK, 128), bf),
            pltpu.VMEM((NP, BLOCK_OUT // 32, 2, 16, 128), bf),
            pltpu.VMEM((NP, BLOCK_IN // 32, 2, 16, 128), bf),
            pltpu.VMEM((TOK, 128), f32),
            pltpu.VMEM((TOK, 128), f32),
            pltpu.VMEM((4, NP, 128), f32),
            pltpu.VMEM((4, NP * NZ, 128), f32),
            pltpu.VMEM((8, NP, 128), f32),
            pltpu.VMEM((8, NP, 128), f32),
            pltpu.VMEM((2, NP, 128), f32),
            pltpu.VMEM((2, NP * NL, 128), f32),
            dma((3,)),
            dma((4,)),
            dma(()),
            dma((NP * NZ,)),
            dma(()),
            dma(()),
            dma(()),
            dma(()),
            dma(()),
            dma(()),
        ],
        compiler_params=pltpu.CompilerParams(
            collective_id=0, has_side_effects=True, vmem_limit_bytes=62 << 20
        ),
        cost_estimate=pl.CostEstimate(
            flops=2 * TOK * 18432 * 64, bytes_accessed=12 << 20, transcendentals=0
        ),
    )(ta, tg, qa, qg, jnp.swapaxes(bo, 1, 2), bi, eig)
    return result.T


def solution(mesh):
    return jax.shard_map(
        per_device,
        mesh=mesh,
        in_specs=(P("layer", "dp", None),) * 6 + (P("layer", None, None),),
        out_specs=P(None, "dp"),
        check_vma=False,
    )
```

```python
import jax
import jax.numpy as jnp
from jax import lax
from jax.experimental import pallas as pl
from jax.experimental.pallas import tpu as pltpu
from jax.sharding import PartitionSpec as P

MESH = pl.DeviceIdType.MESH
NY, NX, NZ = 4, 2, 8
NP = NY * NX
NL = 4
OUT_ROWS, IN_ROWS = 224, 64
PACK_OUT, PACK_IN = OUT_ROWS // 2, IN_ROWS // 2
PACK = PACK_OUT + PACK_IN
CHILDREN = {
    0: (5, 16, 48, 40, 3, 2, 8),
    2: (50, 1, 10, 18),
    3: (11, 19, 51),
    4: (52, 20),
    5: (4, 53, 29, 6, 13, 21),
    6: (14,),
    7: (15,),
    8: (9, 56),
    9: (25, 57),
    11: (27, 59),
    13: (12,),
    16: (23, 24, 32, 17),
    19: (35,),
    21: (22, 37),
    23: (7, 39, 31),
    24: (26,),
    29: (28, 30, 45),
    32: (33,),
    39: (47,),
    40: (46, 41),
    41: (43, 42),
    46: (44,),
    48: (55, 49),
    50: (34, 58),
    52: (36,),
    53: (61,),
    54: (38, 62),
    55: (54,),
    56: (63,),
    61: (60,),
}
ORDER = (
    16, 48, 8, 5, 40, 2, 3, 24, 32, 23, 55, 56, 17, 53, 21, 49,
    4, 13, 9, 50, 29, 6, 51, 18, 46, 10, 41, 1, 11, 19, 7, -1,
    31, 39, 54, 63, 61, 52, 33, -7, 37, 26, 12, 57, 58, 20, 22, -3,
    34, 14, 28, 25, 59, 30, 15, -2, 45, 44, 38, 27, 42, 60, 35, 47,
    36, 62, 43, -6, -8, -5, -4,
)
LATE = 4
STEPS = (
    1, 2, 3, 4, 5, 6, 7,
)
BLOCK_OUT, BLOCK_IN = OUT_ROWS * NZ, IN_ROWS * NZ
TOK_Q, TOK_T = 64, 256
TOK = TOK_Q + TOK_T


def minus(a, b):
    return (
        (a // 16 - b // 16) % NY * 16 + (a // 8 + b // 8) % 2 * 8 + (a - b) % NZ
    )


def body(
    pending, ta, tg, qa, qg, bo, bi, eig, out,
    a_in, a_out, b_o, b_i, eig_v, gath, w_out, w_in, acc_out, acc_in,
    scale, sq, rq, st, rt, sb3, rb3,
    load_sem, act_sem, gsend, grecv, s1, r1, s2, r2, s3, r3,
):
    dp = lax.axis_index("dp")
    layer = lax.axis_index("layer")
    y = dp // 16
    x = lax.rem(dp // 8, 2)
    z = lax.rem(dp, 8)
    k = dp // 8

    small = [
        pltpu.make_async_copy(bo.at[0], b_o, load_sem.at[0]),
        pltpu.make_async_copy(bi.at[0], b_i, load_sem.at[1]),
        pltpu.make_async_copy(eig.at[0], eig_v, load_sem.at[2]),
    ]
    for c in small:
        c.start()

    ys = [lax.rem(y + NY - d, NY) for d in range(NY)]
    xs = [x, 1 - x]
    zs = [lax.rem(z + NZ - d, NZ) for d in range(NZ)]

    def back(d):
        return ys[d // 16] * 16 + xs[d // 8 % 2] * 8 + zs[d % 8]

    def ahead(d):
        return ys[-(d // 16) % NY] * 16 + xs[d // 8 % 2] * 8 + zs[-d % NZ]

    barrier = pltpu.get_barrier_semaphore()
    planes = [lax.rem(k + d, NP) for d in range(NP)]
    layers = [lax.rem(layer + d, NL) for d in range(NL)]
    partners = [(dk, dl) for dk in (4, 5, 2, 6, 3, 7, 1, 0) for dl in (2, 3, 1, 0) if dk or dl]

    def greet(d, ll):
        pl.semaphore_signal(barrier, inc=1, device_id=(d, ll), device_id_type=MESH)

    for d in sorted(STEPS, key=lambda d: abs(d - NZ // 2)):
        greet(back(d), layer)
    for dk, dl in partners:
        greet(planes[dk] * NZ + z, layers[dl])

    acts = [
        pltpu.make_async_copy(qa.at[0], a_in.at[pl.ds(0, TOK_Q)], act_sem.at[0]),
        pltpu.make_async_copy(ta.at[0], a_in.at[pl.ds(TOK_Q, TOK_T)], act_sem.at[1]),
        pltpu.make_async_copy(qg.at[0], a_out.at[pl.ds(0, TOK_Q)], act_sem.at[2]),
        pltpu.make_async_copy(tg.at[0], a_out.at[pl.ds(TOK_Q, TOK_T)], act_sem.at[3]),
    ]

    for c in small[:2]:
        c.wait()
    sb3[...] = jnp.zeros_like(sb3)
    rows = b_o[...].astype(jnp.float32).T.astype(jnp.bfloat16)
    for t in range(PACK_OUT // 16):
        gath[dp, 16 * t : 16 * t + 16, :] = jnp.concatenate(
            [rows[32 * t : 32 * t + 16, :], rows[32 * t + 16 : 32 * t + 32, :]], axis=1
        )
    for t in range(PACK_IN // 16):
        gath[dp, PACK_OUT + 16 * t : PACK_OUT + 16 * t + 16, :] = jnp.concatenate(
            [b_i[32 * t : 32 * t + 16, :], b_i[32 * t + 16 : 32 * t + 32, :]], axis=1
        )

    pl.semaphore_wait(barrier, len(STEPS) + NP * NL - 1)

    def shard_copy(j, to):
        ref = gath.at[j]
        return pltpu.make_async_remote_copy(
            src_ref=ref, dst_ref=ref, send_sem=gsend, recv_sem=grecv.at[j],
            device_id=(to, layer), device_id_type=MESH,
        )

    low = lax.broadcasted_iota(jnp.int32, (PACK_IN, 128), 1) < 64

    def unpack(d, j):
        tile = gath[j, 0:PACK_OUT, :]
        at = pl.ds(zs[d % 8] * (PACK_OUT // 16), PACK_OUT // 16)
        w_out[d // 8, at, 0] = tile.reshape(-1, 16, 128)
        w_out[d // 8, at, 1] = pltpu.roll(tile, 64, 1).reshape(-1, 16, 128)
        tile = gath[j, PACK_OUT:PACK, :]
        turned = pltpu.roll(tile, 64, 1)
        at = pl.ds(zs[d % 8] * (PACK_IN // 16), PACK_IN // 16)
        w_in[d // 8, at, 0] = jnp.where(low, tile, turned).reshape(-1, 16, 128)
        w_in[d // 8, at, 1] = jnp.where(low, turned, tile).reshape(-1, 16, 128)

    def terms(b, tokens):
        kk = ys[b // 2] * NX + xs[b % 2]
        result = []
        for acts, weights, rows in ((a_in, w_in, BLOCK_IN), (a_out, w_out, BLOCK_OUT)):
            cols = pl.ds(pl.multiple_of(kk * rows, 128), rows)
            result.append(
                jnp.dot(
                    acts[tokens, cols], weights[b].reshape(rows, 128),
                    preferred_element_type=jnp.float32,
                )
            )
        return result

    def multiply(b, first):
        for acc, term in zip((acc_in, acc_out), terms(b, slice(0, TOK))):
            acc[...] = term if first else acc[...] + term

    def finish(tokens):
        sums = [acc_in[tokens, :], acc_out[tokens, :]]
        for d in ORDER[len(ORDER) - LATE :]:
            sums = [a + b for a, b in zip(sums, terms(-1 - d, tokens))]
        return [a.astype(jnp.bfloat16) for a in sums]

    queries, trains = slice(0, TOK_Q), slice(TOK_Q, TOK)
    for child in CHILDREN[0]:
        shard_copy(dp, ahead(child)).start()
    for c in acts:
        c.start()
    small[2].wait()
    unpack(0, dp)
    scale[...] = 1.0 / (jnp.concatenate([eig_v[0:32, :], eig_v[32:64, :]], axis=1) + 0.1)
    started = False
    for d in ORDER[: len(ORDER) - LATE]:
        if d < 0:
            if not started:
                for c in acts:
                    c.wait()
            multiply(-1 - d, not started)
            started = True
            continue
        j = back(d)
        shard_copy(j, dp).wait_recv()
        for child in CHILDREN.get(d, ()):
            shard_copy(j, ahead(minus(child, d))).start()
        unpack(d, j)

    every_shard = gath.at[pl.ds(0, NP * NZ - 1)]
    pending.append(
        pltpu.make_async_remote_copy(
            src_ref=every_shard, dst_ref=every_shard, send_sem=gsend, recv_sem=grecv.at[0],
            device_id=(dp, layer), device_id_type=MESH,
        ).wait_send
    )
    half = lax.broadcasted_iota(jnp.int32, (32, 128), 1) < 64

    def outer(right, left):
        full = lax.dot_general(
            left, right, (((0,), (0,)), ((), ())), preferred_element_type=jnp.float32
        )
        return jnp.where(half, full[0:32, :], full[32:64, :]) * (1.0 / left.shape[0])

    def rounded(m):
        return m.astype(jnp.bfloat16).astype(jnp.float32).reshape(4, NP, 128)

    def entries(d, kk):
        return pltpu.make_async_remote_copy(
            src_ref=sq.at[:, kk, :], dst_ref=rq.at[:, dp, :], send_sem=s1, recv_sem=r1,
            device_id=(d, layer), device_id_type=MESH,
        )

    def train_entries(kk):
        return pltpu.make_async_remote_copy(
            src_ref=st.at[:, kk, :], dst_ref=rt.at[:, k, :], send_sem=s2, recv_sem=r2,
            device_id=(kk * NZ + z, layer), device_id_type=MESH,
        )
    sq[...] = rounded(outer(*finish(queries)) * scale[...])
    own_q = pltpu.make_async_copy(sq.at[:, k, :], rq.at[:, dp, :], load_sem.at[0])
    own_q.start()

    for dz in (4, 3, 5, 2, 6, 1, 7, 0):
        def send(n, c, dz=dz):
            kk = lax.rem(k + NP - n, NP)
            entries(kk * NZ + lax.rem(z + dz, NZ), kk).start()
            return c

        lax.fori_loop(1 if dz == 0 else 0, NP, send, 0)

    sides = finish(trains)
    st[0:4] = rounded(outer(*(m[0:128] for m in sides)))
    st[4:8] = rounded(outer(*(m[128:256] for m in sides)))
    own_t = pltpu.make_async_copy(st.at[:, k, :], rt.at[:, k, :], load_sem.at[1])
    own_t.start()

    def send_train(n, c):
        train_entries(lax.rem(k + n, NP)).start()
        return c

    lax.fori_loop(1, NP, send_train, 0)
    own_q.wait()
    own_t.wait()

    def whole(ref, send, recv):
        return pltpu.make_async_remote_copy(
            src_ref=ref, dst_ref=ref, send_sem=send, recv_sem=recv,
            device_id=(dp, layer), device_id_type=MESH,
        )

    some_t = whole(rt.at[:, pl.ds(0, NP - 1), :], s2, r2)
    some_t.wait_recv()
    train = jnp.concatenate(
        [jnp.concatenate([rt[r], rt[4 + r]], axis=0) for r in range(4)], axis=1
    ).astype(jnp.bfloat16)
    some_q = whole(rq.at[:, pl.ds(0, NP * NZ - 1), :], s1, r1)
    some_q.wait_recv()
    pending.append(some_q.wait_send)
    pending.append(some_t.wait_send)
    query = jnp.concatenate([rq[r] for r in range(4)], axis=1).astype(jnp.bfloat16)
    part = lax.dot_general(
        train, query, (((1,), (1,)), ((), ())), preferred_element_type=jnp.float32
    )
    sb3[:, :, 0:64] = part.reshape(2, NP, 64)
    me = k * NL + layer

    own = pltpu.make_async_copy(sb3.at[:, k, :], rb3.at[:, me, :], load_sem.at[2])
    for dk, dl in partners:
        pltpu.make_async_remote_copy(
            src_ref=sb3.at[:, planes[dk], :], dst_ref=rb3.at[:, me, :], send_sem=s3, recv_sem=r3,
            device_id=(planes[dk] * NZ + z, layers[dl]), device_id_type=MESH,
        ).start()
    own.start()
    own.wait()
    some = whole(rb3.at[:, pl.ds(0, NP * NL - 1), :], s3, r3)
    some.wait_recv()
    pending.append(some.wait_send)
    out[...] = jnp.sum(rb3[...], axis=1)[:, 0:64]


def kernel(*refs):
    pending = []
    body(pending, *refs)
    for finish in pending:
        finish()


def per_device(ta, tg, qa, qg, bo, bi, eig):
    any_spec = pl.BlockSpec(memory_space=pl.ANY)
    bf, f32 = jnp.bfloat16, jnp.float32
    dma = pltpu.SemaphoreType.DMA
    result = pl.pallas_call(
        kernel,
        out_shape=pltpu.VMEM((2, 64), f32),
        in_specs=[any_spec] * 7,
        out_specs=pl.BlockSpec(memory_space=pltpu.VMEM),
        scratch_shapes=[
            pltpu.VMEM((TOK, 4096), bf),
            pltpu.VMEM((TOK, 14336), bf),
            pltpu.VMEM((64, OUT_ROWS), bf),
            pltpu.VMEM((IN_ROWS, 64), bf),
            pltpu.VMEM((64, 64), f32),
            pltpu.VMEM((NP * NZ, PACK, 128), bf),
            pltpu.VMEM((NP, BLOCK_OUT // 32, 2, 16, 128), bf),
            pltpu.VMEM((NP, BLOCK_IN // 32, 2, 16, 128), bf),
            pltpu.VMEM((TOK, 128), f32),
            pltpu.VMEM((TOK, 128), f32),
            pltpu.VMEM((32, 128), f32),
            pltpu.VMEM((4, NP, 128), f32),
            pltpu.VMEM((4, NP * NZ, 128), f32),
            pltpu.VMEM((8, NP, 128), f32),
            pltpu.VMEM((8, NP, 128), f32),
            pltpu.VMEM((2, NP, 128), f32),
            pltpu.VMEM((2, NP * NL, 128), f32),
            dma((3,)),
            dma((4,)),
            dma(()),
            dma((NP * NZ,)),
            dma(()),
            dma(()),
            dma(()),
            dma(()),
            dma(()),
            dma(()),
        ],
        compiler_params=pltpu.CompilerParams(
            collective_id=0, has_side_effects=True, vmem_limit_bytes=62 << 20
        ),
        cost_estimate=pl.CostEstimate(
            flops=2 * TOK * 18432 * 64, bytes_accessed=12 << 20, transcendentals=0
        ),
    )(ta, tg, qa, qg, jnp.swapaxes(bo, 1, 2), bi, eig)
    return result.T


def solution(mesh):
    return jax.shard_map(
        per_device,
        mesh=mesh,
        in_specs=(P("layer", "dp", None),) * 6 + (P("layer", None, None),),
        out_specs=P(None, "dp"),
        check_vma=False,
    )
```

```python
import jax
import jax.numpy as jnp
from jax import lax
from jax.experimental import pallas as pl
from jax.experimental.pallas import tpu as pltpu
from jax.sharding import PartitionSpec as P

MESH = pl.DeviceIdType.MESH
NY, NX, NZ = 4, 2, 8
NP = NY * NX
NL = 4
OUT_ROWS, IN_ROWS = 224, 64
PACK_OUT, PACK_IN = OUT_ROWS // 2, IN_ROWS // 2
PACK = PACK_OUT + PACK_IN
CHILDREN = {
    0: (5, 16, 48, 40, 3, 2, 8),
    2: (50, 1, 10, 18),
    3: (11, 19, 51),
    4: (52, 20),
    5: (4, 53, 29, 6, 13, 21),
    6: (14,),
    7: (15,),
    8: (9, 56),
    9: (25, 57),
    11: (27, 59),
    13: (12,),
    16: (23, 24, 32, 17),
    19: (35,),
    21: (22, 37),
    23: (7, 39, 31),
    24: (26,),
    29: (28, 30, 45),
    32: (33,),
    39: (47,),
    40: (46, 41),
    41: (43, 42),
    46: (44,),
    48: (55, 49),
    50: (34, 58),
    52: (36,),
    53: (61,),
    54: (38, 62),
    55: (54,),
    56: (63,),
    61: (60,),
}
ORDER = (
    16, 48, 8, 5, 40, 2, 3, 24, 32, 23, 55, 56, 17, 53, 21, 49,
    4, 13, 9, 50, 29, 6, 51, 18, 46, 10, 41, 1, 11, 19, 7, -1,
    31, 39, 54, 63, 61, 52, 33, -7, 37, 26, 12, 57, 58, 20, 22, -3,
    34, 14, 28, 25, 59, 30, 15, -2, 45, 44, 38, 27, 42, 60, 35, 47,
    36, 62, 43, -6, -8, -5, -4,
)
LATE = 4
STEPS = (
    1, 2, 3, 4, 5, 6, 7,
)
BLOCK_OUT, BLOCK_IN = OUT_ROWS * NZ, IN_ROWS * NZ
TOK_Q, TOK_T = 64, 256
TOK = TOK_Q + TOK_T


def minus(a, b):
    return (
        (a // 16 - b // 16) % NY * 16 + (a // 8 + b // 8) % 2 * 8 + (a - b) % NZ
    )


def body(
    pending, ta, tg, qa, qg, bo, bi, eig, out,
    a_in, a_out, b_o, b_i, eig_v, gath, w_out, w_in, acc_out, acc_in,
    scale, sq, rq, st, rt, sb3, rb3,
    load_sem, act_sem, gsend, grecv, s1, r1, s2, r2, s3, r3,
):
    dp = lax.axis_index("dp")
    layer = lax.axis_index("layer")
    y = dp // 16
    x = lax.rem(dp // 8, 2)
    z = lax.rem(dp, 8)
    k = dp // 8

    small = [
        pltpu.make_async_copy(bo.at[0], b_o, load_sem.at[0]),
        pltpu.make_async_copy(bi.at[0], b_i, load_sem.at[1]),
        pltpu.make_async_copy(eig.at[0], eig_v, load_sem.at[2]),
    ]
    for c in small:
        c.start()

    ys = [lax.rem(y + NY - d, NY) for d in range(NY)]
    xs = [x, 1 - x]
    zs = [lax.rem(z + NZ - d, NZ) for d in range(NZ)]

    def back(d):
        return ys[d // 16] * 16 + xs[d // 8 % 2] * 8 + zs[d % 8]

    def ahead(d):
        return ys[-(d // 16) % NY] * 16 + xs[d // 8 % 2] * 8 + zs[-d % NZ]

    barrier = pltpu.get_barrier_semaphore()
    planes = [lax.rem(k + d, NP) for d in range(NP)]
    layers = [lax.rem(layer + d, NL) for d in range(NL)]
    partners = [(dk, dl) for dk in (4, 5, 2, 6, 3, 7, 1, 0) for dl in (2, 3, 1, 0) if dk or dl]

    def greet(d, ll):
        pl.semaphore_signal(barrier, inc=1, device_id=(d, ll), device_id_type=MESH)

    for d in sorted(STEPS, key=lambda d: abs(d - NZ // 2)):
        greet(back(d), layer)
    for dk, dl in partners:
        greet(planes[dk] * NZ + z, layers[dl])

    acts = [
        pltpu.make_async_copy(qa.at[0], a_in.at[pl.ds(0, TOK_Q)], act_sem.at[0]),
        pltpu.make_async_copy(ta.at[0], a_in.at[pl.ds(TOK_Q, TOK_T)], act_sem.at[1]),
        pltpu.make_async_copy(qg.at[0], a_out.at[pl.ds(0, TOK_Q)], act_sem.at[2]),
        pltpu.make_async_copy(tg.at[0], a_out.at[pl.ds(TOK_Q, TOK_T)], act_sem.at[3]),
    ]

    for c in small[:2]:
        c.wait()
    sb3[...] = jnp.zeros_like(sb3)
    rows = b_o[...].astype(jnp.float32).T.astype(jnp.bfloat16)
    for t in range(PACK_OUT // 16):
        gath[dp, 16 * t : 16 * t + 16, :] = jnp.concatenate(
            [rows[32 * t : 32 * t + 16, :], rows[32 * t + 16 : 32 * t + 32, :]], axis=1
        )
    for t in range(PACK_IN // 16):
        gath[dp, PACK_OUT + 16 * t : PACK_OUT + 16 * t + 16, :] = jnp.concatenate(
            [b_i[32 * t : 32 * t + 16, :], b_i[32 * t + 16 : 32 * t + 32, :]], axis=1
        )

    pl.semaphore_wait(barrier, len(STEPS) + NP * NL - 1)

    def shard_copy(j, to):
        ref = gath.at[j]
        return pltpu.make_async_remote_copy(
            src_ref=ref, dst_ref=ref, send_sem=gsend, recv_sem=grecv.at[j],
            device_id=(to, layer), device_id_type=MESH,
        )

    low = lax.broadcasted_iota(jnp.int32, (PACK_IN, 128), 1) < 64

    def unpack(d, j):
        tile = gath[j, 0:PACK_OUT, :]
        at = pl.ds(zs[d % 8] * (PACK_OUT // 16), PACK_OUT // 16)
        w_out[d // 8, at, 0] = tile.reshape(-1, 16, 128)
        w_out[d // 8, at, 1] = pltpu.roll(tile, 64, 1).reshape(-1, 16, 128)
        tile = gath[j, PACK_OUT:PACK, :]
        turned = pltpu.roll(tile, 64, 1)
        at = pl.ds(zs[d % 8] * (PACK_IN // 16), PACK_IN // 16)
        w_in[d // 8, at, 0] = jnp.where(low, tile, turned).reshape(-1, 16, 128)
        w_in[d // 8, at, 1] = jnp.where(low, turned, tile).reshape(-1, 16, 128)

    def terms(b, tokens):
        kk = ys[b // 2] * NX + xs[b % 2]
        result = []
        for acts, weights, rows in ((a_in, w_in, BLOCK_IN), (a_out, w_out, BLOCK_OUT)):
            cols = pl.ds(pl.multiple_of(kk * rows, 128), rows)
            result.append(
                jnp.dot(
                    acts[tokens, cols], weights[b].reshape(rows, 128),
                    preferred_element_type=jnp.float32,
                )
            )
        return result

    def multiply(b, first):
        for acc, term in zip((acc_in, acc_out), terms(b, slice(0, TOK))):
            acc[...] = term if first else acc[...] + term

    def finish(tokens):
        sums = [acc_in[tokens, :], acc_out[tokens, :]]
        for d in ORDER[len(ORDER) - LATE :]:
            sums = [a + b for a, b in zip(sums, terms(-1 - d, tokens))]
        return [a.astype(jnp.bfloat16) for a in sums]

    queries, trains = slice(0, TOK_Q), slice(TOK_Q, TOK)
    for child in CHILDREN[0]:
        shard_copy(dp, ahead(child)).start()
    for c in acts:
        c.start()
    small[2].wait()
    unpack(0, dp)
    scale[...] = 1.0 / (jnp.concatenate([eig_v[0:32, :], eig_v[32:64, :]], axis=1) + 0.1)
    started = False
    for d in ORDER[: len(ORDER) - LATE]:
        if d < 0:
            if not started:
                for c in acts:
                    c.wait()
            multiply(-1 - d, not started)
            started = True
            continue
        j = back(d)
        shard_copy(j, dp).wait_recv()
        for child in CHILDREN.get(d, ()):
            shard_copy(j, ahead(minus(child, d))).start()
        unpack(d, j)

    every_shard = gath.at[pl.ds(0, NP * NZ - 1)]
    pending.append(
        pltpu.make_async_remote_copy(
            src_ref=every_shard, dst_ref=every_shard, send_sem=gsend, recv_sem=grecv.at[0],
            device_id=(dp, layer), device_id_type=MESH,
        ).wait_send
    )
    half = lax.broadcasted_iota(jnp.int32, (32, 128), 1) < 64

    def outer(right, left):
        full = lax.dot_general(
            left, right, (((0,), (0,)), ((), ())), preferred_element_type=jnp.float32
        )
        return jnp.where(half, full[0:32, :], full[32:64, :]) * (1.0 / left.shape[0])

    def rounded(m):
        return m.astype(jnp.bfloat16).astype(jnp.float32).reshape(4, NP, 128)

    def entries(d, kk):
        return pltpu.make_async_remote_copy(
            src_ref=sq.at[:, kk, :], dst_ref=rq.at[:, dp, :], send_sem=s1, recv_sem=r1,
            device_id=(d, layer), device_id_type=MESH,
        )

    def train_entries(kk):
        return pltpu.make_async_remote_copy(
            src_ref=st.at[:, kk, :], dst_ref=rt.at[:, k, :], send_sem=s2, recv_sem=r2,
            device_id=(kk * NZ + z, layer), device_id_type=MESH,
        )
    sq[...] = rounded(outer(*finish(queries)) * scale[...])
    own_q = pltpu.make_async_copy(sq.at[:, k, :], rq.at[:, dp, :], load_sem.at[0])
    own_q.start()

    for dz in (4, 3, 5, 2, 6, 1, 7, 0):
        for dk in (5, 4, 3, 7, 2, 6, 1, 0):
            if dz or dk:
                entries(planes[dk] * NZ + zs[-dz % NZ], planes[dk]).start()

    sides = finish(trains)
    st[0:4] = rounded(outer(*(m[0:128] for m in sides)))
    st[4:8] = rounded(outer(*(m[128:256] for m in sides)))
    own_t = pltpu.make_async_copy(st.at[:, k, :], rt.at[:, k, :], load_sem.at[1])
    own_t.start()

    for dk in (5, 4, 3, 7, 2, 6, 1):
        train_entries(planes[dk]).start()
    own_q.wait()
    own_t.wait()

    def whole(ref, send, recv):
        return pltpu.make_async_remote_copy(
            src_ref=ref, dst_ref=ref, send_sem=send, recv_sem=recv,
            device_id=(dp, layer), device_id_type=MESH,
        )

    some_t = whole(rt.at[:, pl.ds(0, NP - 1), :], s2, r2)
    some_t.wait_recv()
    train = jnp.concatenate(
        [jnp.concatenate([rt[r], rt[4 + r]], axis=0) for r in range(4)], axis=1
    ).astype(jnp.bfloat16)
    some_q = whole(rq.at[:, pl.ds(0, NP * NZ - 1), :], s1, r1)
    some_q.wait_recv()
    pending.append(some_q.wait_send)
    pending.append(some_t.wait_send)
    query = jnp.concatenate([rq[r] for r in range(4)], axis=1).astype(jnp.bfloat16)
    part = lax.dot_general(
        train, query, (((1,), (1,)), ((), ())), preferred_element_type=jnp.float32
    )
    sb3[:, :, 0:64] = part.reshape(2, NP, 64)
    me = k * NL + layer

    own = pltpu.make_async_copy(sb3.at[:, k, :], rb3.at[:, me, :], load_sem.at[2])
    for dk, dl in partners:
        pltpu.make_async_remote_copy(
            src_ref=sb3.at[:, planes[dk], :], dst_ref=rb3.at[:, me, :], send_sem=s3, recv_sem=r3,
            device_id=(planes[dk] * NZ + z, layers[dl]), device_id_type=MESH,
        ).start()
    own.start()
    own.wait()
    some = whole(rb3.at[:, pl.ds(0, NP * NL - 1), :], s3, r3)
    some.wait_recv()
    pending.append(some.wait_send)
    out[...] = jnp.sum(rb3[...], axis=1)[:, 0:64]


def kernel(*refs):
    pending = []
    body(pending, *refs)
    for finish in pending:
        finish()


def per_device(ta, tg, qa, qg, bo, bi, eig):
    any_spec = pl.BlockSpec(memory_space=pl.ANY)
    bf, f32 = jnp.bfloat16, jnp.float32
    dma = pltpu.SemaphoreType.DMA
    result = pl.pallas_call(
        kernel,
        out_shape=pltpu.VMEM((2, 64), f32),
        in_specs=[any_spec] * 7,
        out_specs=pl.BlockSpec(memory_space=pltpu.VMEM),
        scratch_shapes=[
            pltpu.VMEM((TOK, 4096), bf),
            pltpu.VMEM((TOK, 14336), bf),
            pltpu.VMEM((64, OUT_ROWS), bf),
            pltpu.VMEM((IN_ROWS, 64), bf),
            pltpu.VMEM((64, 64), f32),
            pltpu.VMEM((NP * NZ, PACK, 128), bf),
            pltpu.VMEM((NP, BLOCK_OUT // 32, 2, 16, 128), bf),
            pltpu.VMEM((NP, BLOCK_IN // 32, 2, 16, 128), bf),
            pltpu.VMEM((TOK, 128), f32),
            pltpu.VMEM((TOK, 128), f32),
            pltpu.VMEM((32, 128), f32),
            pltpu.VMEM((4, NP, 128), f32),
            pltpu.VMEM((4, NP * NZ, 128), f32),
            pltpu.VMEM((8, NP, 128), f32),
            pltpu.VMEM((8, NP, 128), f32),
            pltpu.VMEM((2, NP, 128), f32),
            pltpu.VMEM((2, NP * NL, 128), f32),
            dma((3,)),
            dma((4,)),
            dma(()),
            dma((NP * NZ,)),
            dma(()),
            dma(()),
            dma(()),
            dma(()),
            dma(()),
            dma(()),
        ],
        compiler_params=pltpu.CompilerParams(
            collective_id=0, has_side_effects=True, vmem_limit_bytes=62 << 20
        ),
        cost_estimate=pl.CostEstimate(
            flops=2 * TOK * 18432 * 64, bytes_accessed=12 << 20, transcendentals=0
        ),
    )(ta, tg, qa, qg, jnp.swapaxes(bo, 1, 2), bi, eig)
    return result.T


def solution(mesh):
    return jax.shard_map(
        per_device,
        mesh=mesh,
        in_specs=(P("layer", "dp", None),) * 6 + (P("layer", None, None),),
        out_specs=P(None, "dp"),
        check_vma=False,
    )
```
